128 devices in a mesh: section: 8 (over z_lo, x), peer: 16 (over z_hi, y, core).
Axes of the slice: x: 4, y: 4, z: 4 (z_hi: 2, z_lo: 2; z = z_hi * 2 + z_lo), core: 2. Of those that a mesh axis runs over, the one named last changes fastest.
Arguments:
- acts: bfloat16 [8, 256, 5120], P('section', 'peer'), may hold values from -6 to 6
- cotangent: bfloat16 [8, 256, 5120], P('section', 'peer'), may hold values from -6 to 6
- gain: float32 [8, 5120], P('section'), may hold values from 0.25 to 1.75
- w_up: bfloat16 [8, 6912, 5120], P('section', 'peer'), may hold values from -0.078125 to 0.078125
- w_down: bfloat16 [8, 6912, 5120], P('section', 'peer'), may hold values from -0.078125 to 0.078125
- matching: int32 [8, 16], replicated, may hold values from 0 to 15, each once within a row
Outputs:
- grad_acts: bfloat16 [8, 256, 5120], P('section', 'peer')
- second_out: bfloat16 [8, 256, 5120], P('section', 'peer')
- grad_up: bfloat16 [8, 6912, 5120], P('section', 'peer')
- grad_down: bfloat16 [8, 6912, 5120], P('section', 'peer')
- grad_gain: float32 [8, 5120], P('section')
The draws below stay inside these ranges and needn't reach their ends.
Inputs may be any that keep to these rules, and one draw needn't show every extreme that they name: Each row of matching is a permutation of the peers 0 to 15.
All inputs are finite; a program needn't handle non-finite values.
Results may differ from the reference program's by a relative error of at most 0.025.
Values may be sent and summed in bfloat16 or wider, within the bound.
No kernel may reach another device: no remote copies, remote signals or barrier semaphores. Data moves between devices by JAX's collectives and lax.ppermute only.
A program may use at most 128 MiB of HBM per device.

```python
import jax
import jax.numpy as jnp
from jax import lax

D = 5120
HID = 6912
ROWS = 16
TOKENS = 256
N_SECTION = 8
N_PEER = 16


def shard_levels(rng, shape, cuts, least, high):
    level, own = 1.0, jax.random.fold_in(rng, 6)
    for dim, shards_of in cuts:
        steps = jnp.exp(jax.random.uniform(jax.random.fold_in(own, dim), (shards_of,), jnp.float32, least / len(cuts), high / len(cuts)))
        level = level * jnp.repeat(steps, shape[dim] // shards_of).reshape([-1 if axis == dim else 1 for axis in range(len(shape))])
    return level


def noise(rng, shape, width, most, split=(), held_as=jnp.bfloat16):
    entries = jax.random.normal(rng, shape, jnp.float32) * width
    if len(split) > 0:
        entries = shard_levels(rng, shape, split, -0.22, 0.18) * entries
    return jnp.clip(entries, min=-most, max=most).astype(held_as)


def setup_inputs(seed: int = 0) -> dict:
    seeds = jax.random.split(jax.random.key(seed), 7)
    return {
        "acts": noise(seeds[0], (N_SECTION, TOKENS, D), 1.0, 6.0, ((0, 8), (1, 16))),
        "cotangent": noise(seeds[1], (N_SECTION, TOKENS, D), 1.0, 6.0, ((0, 8), (1, 16))),
        "gain": jnp.clip(1.0 + 0.15 * jax.random.normal(seeds[2], (N_SECTION, D), jnp.float32), 0.25, 1.75),
        "w_up": noise(seeds[3], (N_SECTION, HID, D), D ** -0.5, 0.078125, ((0, 8), (1, 16))),
        "w_down": noise(seeds[4], (N_SECTION, HID, D), HID ** -0.5, 0.078125, ((0, 8), (1, 16))),
        "matching": jax.vmap(lambda own: jax.random.permutation(own, N_PEER))(jax.random.split(seeds[5], N_SECTION)).reshape((N_SECTION, N_PEER)).astype(jnp.int32),
    }


def group_sum(left, right):
    group = HID // N_PEER

    def step(total, index):
        piece = lax.dynamic_slice_in_dim(left, index * group, group, 1)
        rows = lax.dynamic_slice_in_dim(right, index * group, group, 0)
        term = jnp.dot(piece, rows, preferred_element_type=jnp.float32).astype(jnp.bfloat16)
        term = lax.optimization_barrier(term)
        return (total + term.astype(jnp.float32), None)
    start = jnp.zeros((left.shape[0], right.shape[1]), jnp.float32)
    total, unused = lax.scan(step, start, jnp.arange(N_PEER, dtype=jnp.int32))
    return total

def forward(rows, gain_row, up, down):
    vf = rows.astype(jnp.float32)
    scale = lax.rsqrt(lax.optimization_barrier(jnp.mean(vf * vf, axis=-1, keepdims=True)) + 1e-05)
    vhat = vf * scale
    normed = (vhat * gain_row).astype(jnp.bfloat16)
    act = lax.dot_general(normed, up, (((1,), (1,)), ((), ())), preferred_element_type=jnp.float32)
    hidden = jax.nn.silu(act).astype(jnp.bfloat16)
    proj = group_sum(hidden, down)
    return ((vf + proj).astype(jnp.bfloat16), (scale, vhat, normed, act, hidden))

def backward(incoming, gain_row, up, down, saved):
    scale, vhat, normed, act, hidden = saved
    d_hidden = lax.dot_general(incoming, down, (((1,), (1,)), ((), ())), preferred_element_type=jnp.float32)
    sigma = jax.nn.sigmoid(act)
    d_act = (d_hidden * sigma * (1.0 + act * (1.0 - sigma))).astype(jnp.bfloat16)
    d_normed = group_sum(d_act, up)
    gain_term = lax.optimization_barrier(jnp.sum(d_normed * vhat, axis=0))
    spread = d_normed * gain_row
    d_rows = incoming.astype(jnp.float32) + scale * (spread - vhat * lax.optimization_barrier(jnp.mean(spread * vhat, axis=-1, keepdims=True)))
    dims = (((0,), (0,)), ((), ()))
    up_term = lax.dot_general(d_act, normed, dims, preferred_element_type=jnp.float32)
    down_term = lax.dot_general(hidden, incoming, dims, preferred_element_type=jnp.float32)
    return (d_rows.astype(jnp.bfloat16), gain_term, up_term, down_term)

def reference(acts, cotangent, gain, w_up, w_down, matching):
    peers = N_PEER
    sections = N_SECTION
    block = ROWS // N_PEER

    def section_forward(inputs):
        rows, gain_row, up, down = inputs
        return forward(rows, gain_row, up, down)[0]
    first = lax.map(section_forward, (acts, gain, w_up, w_down))
    blocks = first.reshape(sections, peers, peers, block, D)
    index_q = jnp.arange(peers, dtype=jnp.int32)

    def route_one(section_id):
        source = jnp.bitwise_xor(index_q[:, None], matching[section_id][None, :])
        return blocks[section_id][index_q[None, :], source]
    moved = lax.map(route_one, jnp.arange(sections - 1, dtype=jnp.int32))
    arrived = jnp.concatenate([jnp.zeros((1, peers, peers, block, D), jnp.bfloat16), moved], axis=0)
    arrived = arrived.reshape(sections, TOKENS, D)

    def section_second(inputs):
        rows, cot_rows, gain_row, up, down = inputs
        out, saved = forward(rows, gain_row, up, down)
        d_rows, gain_term, up_term, down_term = backward(cot_rows, gain_row, up, down, saved)
        return (out, d_rows, gain_term, up_term, down_term)
    second_out, back_arrived, gain_two, up_two, down_two = lax.map(section_second, (arrived, cotangent, gain, w_up, w_down))
    back_blocks = back_arrived.reshape(sections, peers, peers, block, D)

    def return_one(section_id):
        target = jnp.bitwise_xor(index_q[None, :], matching[section_id][:, None])
        return back_blocks[section_id + 1][target, index_q[:, None]]
    returned = lax.map(return_one, jnp.arange(sections - 1, dtype=jnp.int32))
    back_first = jnp.concatenate([returned, jnp.zeros((1, peers, peers, block, D), jnp.bfloat16)], axis=0)
    back_first = back_first.reshape(sections, TOKENS, D)

    def section_first(inputs):
        rows, back_rows, gain_row, up, down = inputs
        out, saved = forward(rows, gain_row, up, down)
        return backward(back_rows, gain_row, up, down, saved)
    grad_acts, gain_one, up_one, down_one = lax.map(section_first, (acts, back_first, gain, w_up, w_down))
    grad_up = (up_one + up_two).astype(jnp.bfloat16)
    grad_down = (down_one + down_two).astype(jnp.bfloat16)
    grad_gain = gain_one + gain_two
    return (grad_acts, second_out, grad_up, grad_down, grad_gain)
```

```python
import functools

import jax
import jax.numpy as jnp
from jax import lax
from jax.experimental import pallas as pl
from jax.experimental.pallas import tpu as pltpu
from jax.sharding import PartitionSpec as P

BF = jnp.bfloat16
F32 = jnp.float32
ROWS = 16
CHIPS = 8
TALL = CHIPS * ROWS
CHUNK = 1024
VMEM_MB = 1024 * 1024

SAME_CORE = [[2 * chip + core for chip in range(CHIPS)] for core in range(2)]
ALONG_Y = [[z * 8 + y * 2 + core for y in range(4)] for z in range(2) for core in range(2)]
ALONG_Z = [[z * 8 + y * 2 + core for z in range(2)] for y in range(4) for core in range(2)]
SIBLING = [(peer, peer ^ 1) for peer in range(16)]

VM = pl.BlockSpec(memory_space=pltpu.VMEM)
SM = pl.BlockSpec(memory_space=pltpu.SMEM)
ANY = pl.BlockSpec(memory_space=pl.ANY)


def dot_nt(left, right):
    return lax.dot_general(left, right, (((1,), (1,)), ((), ())), preferred_element_type=F32)


def dot_nn(left, right):
    return jnp.dot(left, right, preferred_element_type=F32)


def chunks(width):
    return [slice(at, at + CHUNK) for at in range(0, width, CHUNK)]


def row_scale(x_ref):
    rows, width = x_ref.shape
    total = jnp.zeros((rows, 128), F32)
    for at in range(0, width, 128):
        piece = x_ref[:, at : at + 128].astype(F32)
        total = total + piece * piece
    mean = jnp.sum(total, axis=-1, keepdims=True) * (1.0 / width)
    return lax.rsqrt(mean + 1e-05)


class Weights:
    def __init__(self, sources, buffer, sems):
        self.copies = {}
        for at, cols in enumerate(chunks(sources[0].shape[1])):
            for which, source in enumerate(sources):
                copy = pltpu.make_async_copy(source.at[:, cols], buffer.at[which, :, cols], sems.at[at, which])
                copy.start()
                self.copies[at, which] = copy

    def wait(self, at):
        for which in range(2):
            self.copies[at, which].wait()


def silu_parts(act):
    sigma = jax.nn.sigmoid(act)
    return act * sigma, sigma * (1.0 + act * (1.0 - sigma))


def one_hot(index, width):
    lanes = lax.broadcasted_iota(jnp.int32, (index.shape[0], width), 1)
    return jnp.where(lanes == index, 1.0, 0.0).astype(BF)


def forward_kernel(x, gain, up_a, up_b, down_a, down_b, proj, normed, act, hidden, scale_out, wu, wd, su, sd):
    width = x.shape[1]
    ups = Weights((up_a, up_b), wu, su)
    downs = Weights((down_a, down_b), wd, sd)
    scale = row_scale(x)
    scale_out[...] = jnp.broadcast_to(scale, scale_out.shape)
    total = [None, None]
    for at, cols in enumerate(chunks(width)):
        piece = (x[:, cols].astype(F32) * scale * gain[:, cols]).astype(BF)
        normed[:, cols] = piece
        ups.wait(at)
        for half in range(2):
            term = dot_nt(piece, wu[half, :, cols])
            total[half] = term if at == 0 else total[half] + term
    for half in range(2):
        act[half] = total[half]
        hidden[half] = silu_parts(total[half])[0].astype(BF)
    for at, cols in enumerate(chunks(width)):
        downs.wait(at)
        proj[:, cols] = (dot_nn(hidden[0], wd[0, :, cols]) + dot_nn(hidden[1], wd[1, :, cols])).astype(BF)


def cot_kernel(cot_all, pick, down_a, down_b, cot, d_hidden, wd, sd):
    width = cot_all.shape[1]
    downs = Weights((down_a, down_b), wd, sd)
    choose = one_hot(pick[...], cot_all.shape[0])
    total = [None, None]
    for at, cols in enumerate(chunks(width)):
        piece = dot_nn(choose, cot_all[:, cols]).astype(BF)
        cot[:, cols] = piece
        downs.wait(at)
        for half in range(2):
            term = dot_nt(piece, wd[half, :, cols])
            total[half] = term if at == 0 else total[half] + term
    for half in range(2):
        d_hidden[half] = total[half]


def second_kernel(
    x, gain, d_hidden, to_target, own_target, up_a, up_b, down_a, down_b,
    d_normed, proj, normed, d_act, hidden, gain_term, own_rows, wu, wd, su, sd,
):
    width = x.shape[1]
    ups = Weights((up_a, up_b), wu, su)
    downs = Weights((down_a, down_b), wd, sd)
    scale = row_scale(x)
    total = [None, None]
    for at, cols in enumerate(chunks(width)):
        piece = (x[:, cols].astype(F32) * scale * gain[:, cols]).astype(BF)
        normed[:, cols] = piece
        ups.wait(at)
        for half in range(2):
            term = dot_nt(piece, wu[half, :, cols])
            total[half] = term if at == 0 else total[half] + term
    sort = one_hot(to_target[...], TALL)
    own = one_hot(own_target[...], TALL)
    moved = []
    for half in range(2):
        value, slope = silu_parts(total[half])
        rounded = value.astype(BF)
        hidden[half] = rounded
        moved.append(dot_nn(sort, rounded).astype(BF))
        d_act[half] = (d_hidden[half] * slope).astype(BF)
    for at, cols in enumerate(chunks(width)):
        term = dot_nn(d_act[0], wu[0, :, cols]) + dot_nn(d_act[1], wu[1, :, cols])
        d_normed[:, cols] = term.astype(BF)
        gain_term[:, cols] = jnp.sum(term * (x[:, cols].astype(F32) * scale), axis=0, keepdims=True)
    for at, cols in enumerate(chunks(width)):
        downs.wait(at)
        proj[:, cols] = (dot_nn(moved[0], wd[0, :, cols]) + dot_nn(moved[1], wd[1, :, cols])).astype(BF)
        own_rows[:, cols] = dot_nn(own, x[:, cols]).astype(BF)


def first_back_kernel(
    c, x, scale_in, act, gain_two, up_a, up_b, down_a, down_b, d_normed, d_act, wu, wd, su, sd
):
    width = x.shape[1]
    downs = Weights((down_a, down_b), wd, sd)
    ups = Weights((up_a, up_b), wu, su)
    scale = scale_in[:, :1]
    total = [None, None]
    for at, cols in enumerate(chunks(width)):
        downs.wait(at)
        for half in range(2):
            term = dot_nt(c[:, cols], wd[half, :, cols])
            total[half] = term if at == 0 else total[half] + term
    for half in range(2):
        d_act[half] = (total[half] * silu_parts(act[half])[1]).astype(BF)
    gain_pieces = []
    for at, cols in enumerate(chunks(width)):
        ups.wait(at)
        term = dot_nn(d_act[0], wu[0, :, cols]) + dot_nn(d_act[1], wu[1, :, cols])
        d_normed[:, cols] = term.astype(BF)
        gain_pieces.append(
            jnp.sum(term * (x[:, cols].astype(F32) * scale), axis=0, keepdims=True) + gain_two[:, cols]
        )
    line = jnp.concatenate(gain_pieces, axis=1)
    lanes = width // 8
    grid = jnp.concatenate([line[:, lanes * at : lanes * (at + 1)] for at in range(8)], axis=0)
    high = grid.astype(BF)
    low = (grid - high.astype(F32)).astype(BF)
    both = jnp.concatenate([high.astype(F32), low.astype(F32)], axis=0).astype(BF)
    for block in range(CHIPS):
        d_normed[block * ROWS : (block + 1) * ROWS, width:] = both


def add_blocks(blocks, cols):
    total = blocks[0:ROWS, cols].astype(F32)
    for block in range(1, CHIPS):
        total = total + blocks[block * ROWS : (block + 1) * ROWS, cols].astype(F32)
    return total


def add_kernel(blocks, x, out):
    for cols in chunks(x.shape[1]):
        out[:, cols] = (x[:, cols].astype(F32) + add_blocks(blocks, cols)).astype(BF)


def rows_back_kernel(blocks, x, c, gain, *rest):
    out, spread = rest[0], rest[-1]
    width = x.shape[1]
    scale = row_scale(x)
    along = jnp.zeros((ROWS, 128), F32)
    for cols in chunks(width):
        piece = add_blocks(blocks, cols) * gain[:, cols]
        spread[:, cols] = piece
        product = piece * (x[:, cols].astype(F32) * scale)
        for at in range(0, CHUNK, 128):
            along = along + product[:, at : at + 128]
    mean = jnp.sum(along, axis=-1, keepdims=True) * (1.0 / width)
    for cols in chunks(width):
        vhat = x[:, cols].astype(F32) * scale
        out[:, cols] = (c[:, cols].astype(F32) + scale * (spread[:, cols] - vhat * mean)).astype(BF)
    if len(rest) == 3:
        extra = add_blocks(blocks, slice(width, blocks.shape[1]))
        rest[1][...] = extra[:8] + extra[8:]


def grads_kernel(*refs):
    normed, c, d_act, hidden = refs[0:4], refs[4:8], refs[8:12], refs[12:16]
    out_up, out_down, left_up, left_down = refs[16:20]

    @pl.when(pl.program_id(0) == 0)
    def _():
        for at in range(4):
            rows = slice(at * TALL, (at + 1) * TALL)
            left_up[:, rows] = d_act[at][...].T
            left_down[:, rows] = hidden[at][...].T

    right = jnp.concatenate([ref[...] for ref in normed], axis=0)
    out_up[...] = dot_nn(left_up[...], right).astype(BF)
    right = jnp.concatenate([ref[...] for ref in c], axis=0)
    out_down[...] = dot_nn(left_down[...], right).astype(BF)


def shape(*dims, dtype=BF):
    return jax.ShapeDtypeStruct(dims, dtype)


def call(kernel, outs, ins, scratch=(), limit=48, flops=0, moved=0):
    return pl.pallas_call(
        kernel,
        out_shape=outs,
        in_specs=ins,
        out_specs=jax.tree.map(lambda _: VM, outs),
        scratch_shapes=scratch,
        compiler_params=pltpu.CompilerParams(vmem_limit_bytes=limit * VMEM_MB),
        cost_estimate=pl.CostEstimate(flops=flops, bytes_accessed=moved, transcendentals=0),
    )


def weight_scratch(units, width, count):
    steps = width // CHUNK
    return [pltpu.VMEM((2, units, width), BF)] * count + [pltpu.SemaphoreType.DMA((steps, 2))] * count


def to_chips(blocks):
    return lax.all_to_all(
        blocks, "peer", split_axis=0, concat_axis=0, tiled=True, axis_index_groups=SAME_CORE
    )


def from_chips(rows):
    spread = jnp.broadcast_to(rows[None], (CHIPS,) + rows.shape).reshape(TALL, rows.shape[1])
    return to_chips(spread)


def swap(value):
    return lax.ppermute(value, "peer", SIBLING)


def passed_along(value, steps):
    count = lax.axis_size("section")
    leading, last = (max(0, -steps), min(count, count - steps))
    return lax.ppermute(value, "section", [(source, source + steps) for source in range(leading, last)])


def local(acts, cotangent, gain, w_up, w_down, matching):
    section = lax.axis_index("section")
    peer = lax.axis_index("peer")
    core = peer % 2
    chip = peer // 2
    rows_in, up, down = acts[0], w_up[0], w_down[0]
    units, width = up.shape
    flops = 2 * TALL * units * 2 * width
    moved = 2 * units * width * 2

    up_b, down_b = swap(up), swap(down)
    cot_all = lax.all_gather(cotangent[0], "peer", axis=0, tiled=True)

    before = lax.dynamic_index_in_dim(matching, jnp.maximum(section - 1, 0), 0, keepdims=False)
    mine = jnp.where(core == 0, before[0::2], before[1::2])
    chips = jnp.arange(CHIPS, dtype=jnp.int32)
    slots = jnp.arange(ROWS, dtype=jnp.int32)
    pick = (slots[None, :] ^ mine[:, None]) * ROWS + (2 * chips + core)[:, None]
    owner = jnp.array([z * 4 + y for y in range(4) for z in range(2)], jnp.int32)
    to_target = (owner[:, None, None] * 2 + jnp.arange(2, dtype=jnp.int32)[None, :, None]) ^ mine[None, None, :]
    to_target = (to_target + chips[None, None, :] * ROWS).reshape(TALL, 1)
    own_target = (chip * 2 + jnp.arange(2, dtype=jnp.int32))[:, None] ^ mine[None, :]
    own_target = (own_target + chips[None, :] * ROWS).reshape(ROWS, 1)
    pick = pick.reshape(TALL, 1)

    x_one = from_chips(rows_in)
    proj, normed_one, act_one, hidden_one, scale_one = call(
        forward_kernel,
        [shape(TALL, width), shape(TALL, width), shape(2, TALL, units, dtype=F32), shape(2, TALL, units),
         shape(TALL, 128, dtype=F32)],
        [VM, VM, ANY, ANY, ANY, ANY],
        weight_scratch(units, width, 2), flops=2 * flops, moved=2 * moved,
    )(x_one, gain, up, up_b, down, down_b)
    blocks = to_chips(proj)
    first = call(add_kernel, shape(ROWS, width), [VM, VM])(blocks, rows_in)
    arrived = passed_along(first, 1)
    cot, d_hidden = call(
        cot_kernel,
        [shape(TALL, width), shape(2, TALL, units, dtype=F32)],
        [VM, VM, ANY, ANY],
        weight_scratch(units, width, 1), flops=flops, moved=moved,
    )(cot_all, pick, down, down_b)
    x_two = from_chips(arrived)
    d_normed, proj, normed_two, d_act_two, hidden_two, gain_two, own_rows = call(
        second_kernel,
        [shape(TALL, width), shape(TALL, width), shape(TALL, width), shape(2, TALL, units), shape(2, TALL, units),
         shape(1, width, dtype=F32), shape(ROWS, width)],
        [VM] * 5 + [ANY] * 4,
        weight_scratch(units, width, 2), flops=3 * flops, moved=2 * moved,
    )(x_two, gain, d_hidden, to_target, own_target, up, up_b, down, down_b)

    half = lax.psum_scatter(proj, "peer", scatter_dimension=0, tiled=True, axis_index_groups=ALONG_Y)
    total = lax.psum_scatter(half, "peer", scatter_dimension=0, tiled=True, axis_index_groups=ALONG_Z)
    second = (own_rows.astype(F32) + total.astype(F32)).astype(BF).reshape(2, ROWS // 2, width)
    kept = lax.dynamic_index_in_dim(second, core, 0, keepdims=False)
    given = swap(lax.dynamic_index_in_dim(second, 1 - core, 0, keepdims=False))
    even = jnp.where(core == 0, kept, given)
    odd = jnp.where(core == 0, given, kept)
    second = jnp.stack([even, odd], axis=1).reshape(ROWS, width)

    blocks = to_chips(d_normed)
    cot_own = lax.dynamic_slice_in_dim(cot, chip * ROWS, ROWS, 0)
    d_two = call(
        rows_back_kernel, [shape(ROWS, width)], [VM] * 4, [pltpu.VMEM((ROWS, width), F32)]
    )(blocks, arrived, cot_own, gain)[0]
    landed = passed_along(d_two, -1)
    c_one = from_chips(landed)
    d_normed, d_act_one = call(
        first_back_kernel,
        [shape(TALL, width + width // 8), shape(2, TALL, units)],
        [VM] * 5 + [ANY] * 4,
        weight_scratch(units, width, 2), flops=2 * flops, moved=2 * moved,
    )(c_one, x_one, scale_one, act_one, gain_two, up, up_b, down, down_b)
    blocks = to_chips(d_normed)
    d_one, gain_sum = call(
        rows_back_kernel, [shape(ROWS, width), shape(8, width // 8, dtype=F32)], [VM] * 4,
        [pltpu.VMEM((ROWS, width), F32)],
    )(blocks, rows_in, landed, gain)
    grad_gain = (gain_sum + swap(gain_sum)).reshape(1, width)

    wide = [normed_one, swap(normed_one), normed_two, swap(normed_two)]
    wide += [c_one, swap(c_one), cot, swap(cot)]
    slim = [d_act_one[0], swap(d_act_one[1]), d_act_two[0], swap(d_act_two[1])]
    slim += [hidden_one[0], swap(hidden_one[1]), hidden_two[0], swap(hidden_two[1])]
    step = 512
    grad_up, grad_down = pl.pallas_call(
        grads_kernel,
        grid=(width // step,),
        out_shape=[shape(units, width)] * 2,
        in_specs=[pl.BlockSpec((TALL, step), lambda i: (0, i))] * 8 + [VM] * 8,
        out_specs=[pl.BlockSpec((units, step), lambda i: (0, i))] * 2,
        scratch_shapes=[pltpu.VMEM((units, 4 * TALL), BF)] * 2,
        compiler_params=pltpu.CompilerParams(vmem_limit_bytes=32 * VMEM_MB),
        cost_estimate=pl.CostEstimate(flops=4 * flops, bytes_accessed=4 * moved, transcendentals=0),
    )(*wide, *slim)
    return (d_one[None], second[None], grad_up[None], grad_down[None], grad_gain)


def solution(mesh):
    wide = P("section", "peer", None)
    in_specs = (wide, wide, P("section", None), wide, wide, P())
    out_specs = (wide, wide, wide, wide, P("section", None))
    return jax.shard_map(local, mesh=mesh, in_specs=in_specs, out_specs=out_specs, check_vma=False)
```

```python
import jax
import jax.numpy as jnp
from jax import lax
from jax.experimental import pallas as pl
from jax.experimental.pallas import tpu as pltpu
from jax.sharding import PartitionSpec as P

BF = jnp.bfloat16
F32 = jnp.float32
ROWS = 16
CHIPS = 8
TALL = CHIPS * ROWS
CHUNK = 1024
VMEM_MB = 1024 * 1024

SAME_CORE = [[2 * chip + core for chip in range(CHIPS)] for core in range(2)]
SIBLING = [(peer, peer ^ 1) for peer in range(16)]
ACROSS_Z = [(peer, peer ^ 8) for peer in range(16)]
ALONG_Y = [[(peer, peer // 8 * 8 + (peer + 2 * apart) % 8) for peer in range(16)] for apart in range(4)]

VM = pl.BlockSpec(memory_space=pltpu.VMEM)
HBM = pl.BlockSpec(memory_space=pltpu.HBM)


def dot_nt(left, right):
    return lax.dot_general(left, right, (((1,), (1,)), ((), ())), preferred_element_type=F32)


def dot_nn(left, right):
    return jnp.dot(left, right, preferred_element_type=F32)


def chunks(width):
    return [slice(at, at + CHUNK) for at in range(0, width, CHUNK)]


def row_scale(x_ref):
    rows, width = x_ref.shape
    total = jnp.zeros((rows, 128), F32)
    for at in range(0, width, 128):
        piece = x_ref[:, at : at + 128].astype(F32)
        total = total + piece * piece
    mean = jnp.sum(total, axis=-1, keepdims=True) * (1.0 / width)
    return lax.rsqrt(mean + 1e-05)


def silu_parts(act):
    sigma = jax.nn.sigmoid(act)
    return act * sigma, sigma * (1.0 + act * (1.0 - sigma))


def one_hot(index, width):
    lanes = lax.broadcasted_iota(jnp.int32, (index.shape[0], width), 1)
    return jnp.where(lanes == index, 1.0, 0.0).astype(BF)


class Weights:
    def __init__(self, sources, buffer, sems):
        self.copies = []
        for at, cols in enumerate(chunks(sources[0].shape[1])):
            self.copies.append(
                [
                    pltpu.make_async_copy(source.at[:, cols], buffer.at[which, :, cols], sems.at[at, which])
                    for which, source in enumerate(sources)
                ]
            )

    def start(self, at):
        for copy in self.copies[at]:
            copy.start()

    def start_all(self):
        for at in range(len(self.copies)):
            self.start(at)

    def wait(self, at):
        for copy in self.copies[at]:
            copy.wait()


class Stores:
    def __init__(self, sems):
        self.sems = sems
        self.copies = []

    def add(self, source, target):
        copy = pltpu.make_async_copy(source, target, self.sems.at[len(self.copies)])
        copy.start()
        self.copies.append(copy)

    def finish(self):
        for copy in self.copies:
            copy.wait()


def normed_times_up(x, scale, gain, normed, normed_out, stores, ups, wu, following=None):
    total = [None, None]
    for at, cols in enumerate(chunks(x.shape[1])):
        piece = (x[:, cols].astype(F32) * scale * gain[:, cols]).astype(BF)
        normed[:, cols] = piece
        stores.add(normed.at[:, cols], normed_out.at[:, cols])
        ups.wait(at)
        if following is not None:
            following.start(at)
        for half in range(2):
            term = dot_nt(piece, wu[half, :, cols])
            total[half] = term if at == 0 else total[half] + term
    return total


def forward_kernel(
    x, gain, up_a, up_b, down_a, down_b,
    proj, normed_out, slope_out, hidden_a_out, hidden_b_out,
    wu, wd, su, sd, normed, slope, hidden, so,
):
    ups = Weights((up_a, up_b), wu, su)
    downs = Weights((down_a, down_b), wd, sd)
    ups.start_all()
    stores = Stores(so)
    scale = row_scale(x)
    total = normed_times_up(x, scale, gain, normed, normed_out, stores, ups, wu, downs)
    for half in range(2):
        value, slant = silu_parts(total[half])
        slope[half] = slant
        hidden[half] = value.astype(BF)
    stores.add(slope, slope_out)
    stores.add(hidden.at[0], hidden_a_out)
    stores.add(hidden.at[1], hidden_b_out)
    for at, cols in enumerate(chunks(x.shape[1])):
        downs.wait(at)
        proj[:, cols] = (dot_nn(hidden[0], wd[0, :, cols]) + dot_nn(hidden[1], wd[1, :, cols])).astype(BF)
    stores.finish()


def pick_kernel(*refs):
    sources, index, out = refs[:-2], refs[-2], refs[-1]
    choose = one_hot(index[...], len(sources) * ROWS)
    for cols in chunks(out.shape[1]):
        rows = jnp.concatenate([source[:, cols] for source in sources], axis=0)
        out[:, cols] = dot_nn(choose, rows).astype(BF)


def join_kernel(own, even, odd, third, fourth, first_pair, second_pair):
    first_pair[:ROWS, :] = own[...]
    first_pair[ROWS:, :] = even[...] + odd[...]
    second_pair[:ROWS, :] = third[...]
    second_pair[ROWS:, :] = fourth[...]


def spread_kernel(rows, out):
    for at in range(0, out.shape[0], ROWS):
        out[at : at + ROWS, :] = rows[...]


def cot_kernel(*refs):
    sources, (pick, own_pick, down_a, down_b) = refs[:4], refs[4:8]
    cot_own, cot_out, d_hidden_out, wd, sd, cot, d_hidden, so = refs[8:]
    downs = Weights((down_a, down_b), wd, sd)
    downs.start_all()
    stores = Stores(so)
    choose = one_hot(pick[...], TALL)
    own = one_hot(own_pick[...], TALL)
    total = [None, None]
    for at, cols in enumerate(chunks(cot.shape[1])):
        rows = jnp.concatenate([source[:, cols] for source in sources], axis=0)
        piece = dot_nn(choose, rows).astype(BF)
        cot[:, cols] = piece
        stores.add(cot.at[:, cols], cot_out.at[:, cols])
        cot_own[:, cols] = dot_nn(own, piece).astype(BF)
        downs.wait(at)
        for half in range(2):
            term = dot_nt(piece, wd[half, :, cols])
            total[half] = term if at == 0 else total[half] + term
    for half in range(2):
        d_hidden[half] = total[half]
    stores.add(d_hidden, d_hidden_out)
    stores.finish()


def second_kernel(
    x, gain, own_target, d_hidden_in, up_a, up_b,
    gain_term, own_rows, dn, normed_out, d_act_a_out, d_act_b_out, hidden_a_out, hidden_b_out,
    wu, su, normed, d_act, hidden, d_hidden, sh, so,
):
    ups = Weights((up_a, up_b), wu, su)
    ups.start_all()
    fetch = pltpu.make_async_copy(d_hidden_in, d_hidden, sh)
    fetch.start()
    stores = Stores(so)
    scale = row_scale(x)
    total = normed_times_up(x, scale, gain, normed, normed_out, stores, ups, wu)
    fetch.wait()
    for half in range(2):
        value, slope = silu_parts(total[half])
        hidden[half] = value.astype(BF)
        d_act[half] = (d_hidden[half] * slope).astype(BF)
    stores.add(d_act.at[0], d_act_a_out)
    stores.add(d_act.at[1], d_act_b_out)
    stores.add(hidden.at[0], hidden_a_out)
    stores.add(hidden.at[1], hidden_b_out)
    own = one_hot(own_target[...], TALL)
    for cols in chunks(x.shape[1]):
        term = dot_nn(d_act[0], wu[0, :, cols]) + dot_nn(d_act[1], wu[1, :, cols])
        dn[:, cols] = term.astype(BF)
        gain_term[:, cols] = jnp.sum(term * normed[:, cols].astype(F32), axis=0, keepdims=True) / gain[:, cols]
        own_rows[:, cols] = dot_nn(own, x[:, cols]).astype(BF)
    stores.finish()


def target_kernel(to_target, hidden_a, hidden_b, down_a, down_b, near, second, third, fourth, wd, sd, hidden, sh):
    fetches = [pltpu.make_async_copy(ref, hidden.at[at], sh.at[at]) for at, ref in enumerate((hidden_a, hidden_b))]
    for fetch in fetches:
        fetch.start()
    downs = Weights((down_a, down_b), wd, sd)
    downs.start_all()
    sort = one_hot(to_target[...], TALL)
    left = []
    for half, fetch in enumerate(fetches):
        fetch.wait()
        left.append(dot_nn(sort, hidden[half]).astype(BF))
    for at, cols in enumerate(chunks(near.shape[1])):
        downs.wait(at)
        term = (dot_nn(left[0], wd[0, :, cols]) + dot_nn(left[1], wd[1, :, cols])).astype(BF)
        for part, out in enumerate((near, second, third, fourth)):
            out[:, cols] = term[2 * ROWS * part : 2 * ROWS * (part + 1)]


def sum_kernel(near, second, third, fourth, mine, other):
    for cols in chunks(near.shape[1]):
        total = near[:, cols].astype(F32) + second[:, cols].astype(F32)
        total = total + (third[:, cols].astype(F32) + fourth[:, cols].astype(F32))
        mine[:, cols] = total[:ROWS]
        other[:, cols] = total[ROWS:].astype(BF)


def second_out_kernel(own_rows, mine, given, out):
    for cols in chunks(out.shape[1]):
        out[:, cols] = (own_rows[:, cols].astype(F32) + (mine[:, cols] + given[:, cols].astype(F32))).astype(BF)


def first_back_kernel(
    c, gain, gain_two, slope_in, normed_in, up_a, up_b, down_a, down_b,
    dn, c_out, d_act_a_out, d_act_b_out,
    wu, wd, su, sd, d_act, slope, normed, sh, so,
):
    width = c.shape[1]
    downs = Weights((down_a, down_b), wd, sd)
    ups = Weights((up_a, up_b), wu, su)
    downs.start_all()
    fetches = [pltpu.make_async_copy(slope_in, slope, sh.at[0]), pltpu.make_async_copy(normed_in, normed, sh.at[1])]
    stores = Stores(so)
    stores.add(c, c_out)
    total = [None, None]
    for at, cols in enumerate(chunks(width)):
        downs.wait(at)
        if at == 0:
            for fetch in fetches:
                fetch.start()
        ups.start(at)
        for half in range(2):
            term = dot_nt(c[:, cols], wd[half, :, cols])
            total[half] = term if at == 0 else total[half] + term
    for fetch in fetches:
        fetch.wait()
    for half in range(2):
        d_act[half] = (total[half] * slope[half]).astype(BF)
    stores.add(d_act.at[0], d_act_a_out)
    stores.add(d_act.at[1], d_act_b_out)
    gain_pieces = []
    for at, cols in enumerate(chunks(width)):
        ups.wait(at)
        term = dot_nn(d_act[0], wu[0, :, cols]) + dot_nn(d_act[1], wu[1, :, cols])
        dn[:, cols] = term.astype(BF)
        product = jnp.sum(term * normed[:, cols].astype(F32), axis=0, keepdims=True)
        gain_pieces.append(product / gain[:, cols] + gain_two[:, cols])
    line = jnp.concatenate(gain_pieces, axis=1)
    lanes = width // 8
    grid = jnp.concatenate([line[:, lanes * at : lanes * (at + 1)] for at in range(8)], axis=0)
    high = grid.astype(BF).astype(F32)
    both = jnp.concatenate([high, grid - high], axis=0).astype(BF)
    for block in range(CHIPS):
        dn[block * ROWS : (block + 1) * ROWS, width:] = both
    stores.finish()


def add_blocks(blocks, cols):
    total = blocks[0:ROWS, cols].astype(F32)
    for at in range(ROWS, blocks.shape[0], ROWS):
        total = total + blocks[at : at + ROWS, cols].astype(F32)
    return total


def add_kernel(blocks, x, out):
    for cols in chunks(x.shape[1]):
        out[:, cols] = (x[:, cols].astype(F32) + add_blocks(blocks, cols)).astype(BF)


def rows_back_kernel(blocks, x, c, gain, *rest):
    out, spread = rest[0], rest[-1]
    width = x.shape[1]
    scale = row_scale(x)
    along = jnp.zeros((ROWS, 128), F32)
    for cols in chunks(width):
        piece = add_blocks(blocks, cols) * gain[:, cols]
        spread[:, cols] = piece
        product = piece * (x[:, cols].astype(F32) * scale)
        for at in range(0, CHUNK, 128):
            along = along + product[:, at : at + 128]
    mean = jnp.sum(along, axis=-1, keepdims=True) * (1.0 / width)
    for cols in chunks(width):
        vhat = x[:, cols].astype(F32) * scale
        out[:, cols] = (c[:, cols].astype(F32) + scale * (spread[:, cols] - vhat * mean)).astype(BF)
    if len(rest) == 3:
        extra = add_blocks(blocks, slice(width, blocks.shape[1]))
        line = extra[:8] + extra[8:]
        rest[1][...] = jnp.concatenate([line[at : at + 1] for at in range(8)], axis=1)


def grads_kernel(*refs):
    normed, c, slim = refs[0:4], refs[4:8], refs[8:16]
    out_up, out_down, left_up, left_down, held, sems = refs[16:22]

    @pl.when(pl.program_id(0) == 0)
    def _():
        copies = [pltpu.make_async_copy(ref, held.at[at], sems.at[at]) for at, ref in enumerate(slim)]
        for copy in copies:
            copy.start()
        for at in range(4):
            rows = slice(at * TALL, (at + 1) * TALL)
            copies[at].wait()
            left_up[:, rows] = held[at].T
            copies[4 + at].wait()
            left_down[:, rows] = held[4 + at].T

    right = jnp.concatenate([ref[...] for ref in normed], axis=0)
    out_up[...] = dot_nn(left_up[...], right).astype(BF)
    right = jnp.concatenate([ref[...] for ref in c], axis=0)
    out_down[...] = dot_nn(left_down[...], right).astype(BF)


def in_vmem(*dims, dtype=BF):
    return pltpu.VMEM(dims, dtype)


def shape(*dims, dtype=BF):
    return jax.ShapeDtypeStruct(dims, dtype)


def in_hbm(value):
    return pltpu.with_memory_space_constraint(value, pltpu.HBM)


def call(kernel, outs, args, from_hbm=(), hbm_outs=(), scratch=(), limit=16, flops=0, moved=0):
    return pl.pallas_call(
        kernel,
        out_shape=list(outs) + [pltpu.HBM(out.shape, out.dtype) for out in hbm_outs],
        in_specs=[VM] * len(args) + [HBM] * len(from_hbm),
        out_specs=[VM] * len(outs) + [HBM] * len(hbm_outs),
        scratch_shapes=scratch,
        compiler_params=pltpu.CompilerParams(vmem_limit_bytes=limit * VMEM_MB),
        cost_estimate=pl.CostEstimate(flops=flops, bytes_accessed=moved, transcendentals=0),
    )(*args, *[in_hbm(value) for value in from_hbm])


def kept(*dims, dtype=BF):
    return pltpu.VMEM(dims, dtype)


def dma(*dims):
    return pltpu.SemaphoreType.DMA(dims)


def weight_scratch(units, width, count):
    return [kept(2, units, width)] * count + [dma(width // CHUNK, 2)] * count


def to_chips(blocks):
    return lax.all_to_all(
        blocks, "peer", split_axis=0, concat_axis=0, tiled=True, axis_index_groups=SAME_CORE
    )


def from_chips(rows):
    width = rows.shape[1]
    return to_chips(call(spread_kernel, [in_vmem(TALL, width)], [rows], limit=4, moved=TALL * width * 4)[0])


def swap(value):
    return lax.ppermute(value, "peer", SIBLING)


def after(value, *earlier):
    return lax.optimization_barrier((value,) + earlier)[0]


def together(*values):
    return lax.optimization_barrier(values)


def passed_along(value, steps):
    count = lax.axis_size("section")
    leading, last = (max(0, -steps), min(count, count - steps))
    return lax.ppermute(value, "section", [(source, source + steps) for source in range(leading, last)])


def local(acts, cotangent, gain, w_up, w_down, matching):
    section = lax.axis_index("section")
    peer = lax.axis_index("peer")
    core = peer % 2
    chip = peer // 2
    rows_in, cot_in, up, down = acts[0], cotangent[0], w_up[0], w_down[0]
    units, width = up.shape
    flops = 4 * TALL * units * width
    moved = 2 * TALL * width * 2
    steps = width // CHUNK
    tall, block, slim = shape(TALL, width), shape(ROWS, width), shape(TALL, units)
    pair_f32 = shape(2, TALL, units, dtype=F32)

    cot_b = swap(cot_in)
    up_b, down_b = swap(after(up, cot_b)), swap(after(down, cot_b))

    before = lax.dynamic_index_in_dim(matching, jnp.maximum(section - 1, 0), 0, keepdims=False)
    mine = jnp.where(core == 0, before[0::2], before[1::2])
    chips = jnp.arange(CHIPS, dtype=jnp.int32)
    slots = jnp.arange(ROWS, dtype=jnp.int32)
    pair = jnp.arange(2, dtype=jnp.int32)
    wanted = slots[None, :] ^ mine[:, None]
    apart_y, apart_z = (wanted // 2 - chip) % 4, (wanted // 8) ^ (chip // 4)
    pick = ((apart_z * 4 + apart_y) * ROWS + (wanted % 2) * CHIPS + chips[:, None]).reshape(TALL, 1)
    cot_index = (jnp.where(pair == core, 0, ROWS)[:, None] + 2 * chips[None, :] + core).reshape(ROWS, 1)
    owner = (((chip // 4) ^ pair) * 4)[None, :] + ((chip + jnp.arange(4, dtype=jnp.int32)) % 4)[:, None]
    to_target = (owner.reshape(CHIPS, 1, 1) * 2 + pair[None, :, None]) ^ mine[None, None, :]
    to_target = (to_target + chips[None, None, :] * ROWS).reshape(TALL, 1)
    own_target = to_target[:ROWS]
    own_pick = (chip * ROWS + slots).reshape(ROWS, 1)
    out_index = (jnp.where(slots % 2 == core, 0, ROWS) + core * CHIPS + slots // 2).reshape(ROWS, 1)

    cot_half = call(pick_kernel, [block], [cot_in, cot_b, cot_index], moved=moved // 4)[0]
    even = lax.ppermute(cot_half, "peer", ALONG_Y[3][0::2])
    x_one = from_chips(after(rows_in, even))
    rest = after(cot_half, even)
    cot_y = [lax.ppermute(rest, "peer", pairs) for pairs in (ALONG_Y[3][1::2], ALONG_Y[2], ALONG_Y[1])]
    cot_a, cot_b = call(join_kernel, [shape(2 * ROWS, width)] * 2, [cot_half, even] + cot_y, moved=moved)
    x_one, cot_a, cot_b = together(x_one, cot_a, cot_b)
    cot_za = lax.ppermute(cot_a, "peer", ACROSS_Z)
    proj, normed_one, slope_one, hidden_one, hidden_one_b = call(
        forward_kernel, [in_vmem(TALL, width)], [x_one, gain], [up, up_b, down, down_b], [tall, pair_f32, slim, slim],
        weight_scratch(units, width, 2)
        + [kept(TALL, width), kept(2, TALL, units, dtype=F32), kept(2, TALL, units), dma(steps + 3)],
        limit=36, flops=3 * flops, moved=6 * moved,
    )
    proj, cot_za = together(proj, cot_za)
    blocks = to_chips(proj)
    first = call(add_kernel, [block], [blocks, rows_in], moved=moved)[0]
    arrived = passed_along(first, 1)
    cot_zb = lax.ppermute(after(cot_b, first), "peer", ACROSS_Z)
    arrived, cot_zb = together(arrived, cot_zb)
    cot_all = [cot_a, cot_b, cot_za, cot_zb]
    x_two = from_chips(arrived)
    cot_own, cot, d_hidden = call(
        cot_kernel, [block], cot_all + [pick, own_pick], [down, down_b], [tall, pair_f32],
        weight_scratch(units, width, 1) + [kept(TALL, width), kept(2, TALL, units, dtype=F32), dma(steps + 1)],
        limit=20, flops=3 * flops, moved=3 * moved,
    )
    gain_two, own_rows, d_normed, normed_two, d_act_two, d_act_two_b, hidden_two, hidden_two_b = call(
        second_kernel, [shape(1, width, dtype=F32), block, in_vmem(TALL, width)],
        [x_two, gain, own_target], [d_hidden, up, up_b], [tall, slim, slim, slim, slim],
        weight_scratch(units, width, 1)
        + [kept(TALL, width), kept(2, TALL, units), kept(2, TALL, units), kept(2, TALL, units, dtype=F32),
           pltpu.SemaphoreType.DMA, dma(steps + 4)],
        limit=28, flops=3 * flops, moved=4 * moved,
    )
    blocks = to_chips(d_normed)
    parts = call(
        target_kernel, [shape(2 * ROWS, width)] * 4, [to_target], [hidden_two, hidden_two_b, down, down_b], [],
        weight_scratch(units, width, 1) + [kept(2, TALL, units), dma(2)],
        limit=20, flops=2 * flops, moved=3 * moved,
    )
    d_two = call(
        rows_back_kernel, [block], [blocks, arrived, cot_own, gain], scratch=[kept(ROWS, width, dtype=F32)], moved=moved
    )[0]
    landed = passed_along(d_two, -1)
    near = together(*parts, d_two)
    part_up, part_down = lax.ppermute(near[1], "peer", ALONG_Y[1]), lax.ppermute(near[3], "peer", ALONG_Y[3])
    landed, part_up, part_down = together(landed, part_up, part_down)
    c_all = from_chips(landed)
    c_all, far = together(c_all, parts[2])
    part_far = lax.ppermute(far, "peer", ALONG_Y[2])
    d_normed, c_one, d_act_one, d_act_one_b = call(
        first_back_kernel, [in_vmem(TALL, width + width // 8)], [c_all, gain, gain_two],
        [slope_one, normed_one, up, up_b, down, down_b], [tall, slim, slim],
        weight_scratch(units, width, 2)
        + [kept(2, TALL, units), kept(2, TALL, units, dtype=F32), kept(TALL, width), dma(2), dma(3)],
        limit=36, flops=3 * flops, moved=6 * moved,
    )
    d_normed, part_far = together(d_normed, part_far)
    blocks = to_chips(d_normed)
    own_part, other_part = call(
        sum_kernel, [shape(ROWS, width, dtype=F32), block], [parts[0], part_up, part_far, part_down], moved=moved
    )
    given = lax.ppermute(after(other_part, d_normed), "peer", ACROSS_Z)
    wide, thin = [], []
    for value in (normed_one, normed_two, c_one, cot):
        wide += [value, swap(after(value, d_normed))]
    for own, other in ((d_act_one, d_act_one_b), (d_act_two, d_act_two_b), (hidden_one, hidden_one_b), (hidden_two, hidden_two_b)):
        thin += [own, swap(after(other, d_normed))]
    step = 1024
    grad_up, grad_down = pl.pallas_call(
        grads_kernel,
        grid=(width // step,),
        out_shape=[shape(units, width)] * 2,
        in_specs=[pl.BlockSpec((TALL, step), lambda i: (0, i))] * 8 + [HBM] * 8,
        out_specs=[pl.BlockSpec((units, step), lambda i: (0, i))] * 2,
        scratch_shapes=[kept(units, 4 * TALL)] * 2 + [kept(8, TALL, units), dma(8)],
        compiler_params=pltpu.CompilerParams(vmem_limit_bytes=24 * VMEM_MB),
        cost_estimate=pl.CostEstimate(flops=4 * flops, bytes_accessed=8 * moved, transcendentals=0),
    )(*[in_hbm(value) for value in wide], *[in_hbm(value) for value in thin])

    d_one, gain_sum = call(
        rows_back_kernel, [block, shape(1, width, dtype=F32)], [after(blocks, grad_up), rows_in, landed, gain],
        scratch=[kept(ROWS, width, dtype=F32)], moved=moved,
    )
    second = call(second_out_kernel, [block], [after(own_rows, grad_up), own_part, given], moved=moved // 4)[0]
    second = call(pick_kernel, [block], [second, swap(second), out_index])[0]
    grad_gain = gain_sum + swap(gain_sum)
    return (d_one[None], second[None], grad_up[None], grad_down[None], grad_gain)


def solution(mesh):
    wide = P("section", "peer", None)
    in_specs = (wide, wide, P("section", None), wide, wide, P())
    out_specs = (wide, wide, wide, wide, P("section", None))
    return jax.shard_map(local, mesh=mesh, in_specs=in_specs, out_specs=out_specs, check_vma=False)
```

```python
import jax
import jax.numpy as jnp
from jax import lax
from jax.experimental import pallas as pl
from jax.experimental.pallas import tpu as pltpu
from jax.sharding import PartitionSpec as P

BF = jnp.bfloat16
F32 = jnp.float32
ROWS = 16
CHIPS = 8
TALL = CHIPS * ROWS
CHUNK = 1024
VMEM_MB = 1024 * 1024

SAME_CORE = [[2 * chip + core for chip in range(CHIPS)] for core in range(2)]
SIBLING = [(peer, peer ^ 1) for peer in range(16)]
ACROSS_Z = [(peer, peer ^ 8) for peer in range(16)]
ALONG_Y = [[(peer, peer // 8 * 8 + (peer + 2 * apart) % 8) for peer in range(16)] for apart in range(4)]

VM = pl.BlockSpec(memory_space=pltpu.VMEM)
HBM = pl.BlockSpec(memory_space=pltpu.HBM)


def dot_nt(left, right):
    return lax.dot_general(left, right, (((1,), (1,)), ((), ())), preferred_element_type=F32)


def dot_nn(left, right):
    return jnp.dot(left, right, preferred_element_type=F32)


def chunks(width):
    return [slice(at, at + CHUNK) for at in range(0, width, CHUNK)]


def row_scale(x_ref):
    rows, width = x_ref.shape
    total = jnp.zeros((rows, 128), F32)
    for at in range(0, width, 128):
        piece = x_ref[:, at : at + 128].astype(F32)
        total = total + piece * piece
    mean = jnp.sum(total, axis=-1, keepdims=True) * (1.0 / width)
    return lax.rsqrt(mean + 1e-05)


def silu_parts(act):
    sigma = jax.nn.sigmoid(act)
    return act * sigma, sigma * (1.0 + act * (1.0 - sigma))


def one_hot(index, width):
    lanes = lax.broadcasted_iota(jnp.int32, (index.shape[0], width), 1)
    return jnp.where(lanes == index, 1.0, 0.0).astype(BF)


class Weights:
    def __init__(self, sources, buffer, sems):
        self.copies = []
        for at, cols in enumerate(chunks(sources[0].shape[1])):
            self.copies.append(
                [
                    pltpu.make_async_copy(source.at[:, cols], buffer.at[which, :, cols], sems.at[at, which])
                    for which, source in enumerate(sources)
                ]
            )

    def start(self, at):
        for copy in self.copies[at]:
            copy.start()

    def start_all(self):
        for at in range(len(self.copies)):
            self.start(at)

    def wait(self, at):
        for copy in self.copies[at]:
            copy.wait()


class Stores:
    def __init__(self, sems):
        self.sems = sems
        self.copies = []

    def add(self, source, target):
        copy = pltpu.make_async_copy(source, target, self.sems.at[len(self.copies)])
        copy.start()
        self.copies.append(copy)

    def finish(self):
        for copy in self.copies:
            copy.wait()


def normed_times_up(x, scale, gain, normed, normed_out, stores, ups, wu, following=None):
    total = [None, None]
    for at, cols in enumerate(chunks(x.shape[1])):
        piece = (x[:, cols].astype(F32) * scale * gain[:, cols]).astype(BF)
        normed[:, cols] = piece
        stores.add(normed.at[:, cols], normed_out.at[:, cols])
        ups.wait(at)
        if following is not None:
            following.start(at)
        for half in range(2):
            term = dot_nt(piece, wu[half, :, cols])
            total[half] = term if at == 0 else total[half] + term
    return total


def forward_kernel(
    x, gain, up_a, up_b, down_a, down_b,
    proj, normed_out, slope_out, hidden_a_out, hidden_b_out,
    wu, wd, su, sd, normed, slope, hidden, so,
):
    ups = Weights((up_a, up_b), wu, su)
    downs = Weights((down_a, down_b), wd, sd)
    ups.start_all()
    stores = Stores(so)
    scale = row_scale(x)
    total = normed_times_up(x, scale, gain, normed, normed_out, stores, ups, wu, downs)
    for half in range(2):
        value, slant = silu_parts(total[half])
        slope[half] = slant
        hidden[half] = value.astype(BF)
    stores.add(slope, slope_out)
    stores.add(hidden.at[0], hidden_a_out)
    stores.add(hidden.at[1], hidden_b_out)
    for at, cols in enumerate(chunks(x.shape[1])):
        downs.wait(at)
        proj[:, cols] = (dot_nn(hidden[0], wd[0, :, cols]) + dot_nn(hidden[1], wd[1, :, cols])).astype(BF)
    stores.finish()


def pick_kernel(*refs):
    sources, index, out = refs[:-2], refs[-2], refs[-1]
    choose = one_hot(index[...], len(sources) * ROWS)
    for cols in chunks(out.shape[1]):
        rows = jnp.concatenate([source[:, cols] for source in sources], axis=0)
        out[:, cols] = dot_nn(choose, rows).astype(BF)


def join_kernel(own, even, odd, third, fourth, first_pair, second_pair):
    first_pair[:ROWS, :] = own[...]
    first_pair[ROWS:, :] = even[...] + odd[...]
    second_pair[:ROWS, :] = third[...]
    second_pair[ROWS:, :] = fourth[...]


def prepare_kernel(other, index, rows, own_in, wide, share, own, sem, sems):
    fetch = pltpu.make_async_copy(own_in, own, sem)
    fetch.start()
    copies = []
    for at in range(CHIPS):
        copies.append(pltpu.make_async_copy(rows, wide.at[at * ROWS : (at + 1) * ROWS, :], sems.at[at]))
        copies[-1].start()
    fetch.wait()
    pick_kernel(own, other, index, share)
    for copy in copies:
        copy.wait()


def spread_kernel(rows, out):
    for at in range(0, out.shape[0], ROWS):
        out[at : at + ROWS, :] = rows[...]


def cot_kernel(*refs):
    sources, (pick, own_pick, down_a, down_b) = refs[:4], refs[4:8]
    cot_own, cot_out, d_hidden_out, wd, sd, cot, d_hidden, so = refs[8:]
    downs = Weights((down_a, down_b), wd, sd)
    downs.start_all()
    stores = Stores(so)
    choose = one_hot(pick[...], TALL)
    own = one_hot(own_pick[...], TALL)
    total = [None, None]
    for at, cols in enumerate(chunks(cot.shape[1])):
        rows = jnp.concatenate([source[:, cols] for source in sources], axis=0)
        piece = dot_nn(choose, rows).astype(BF)
        cot[:, cols] = piece
        stores.add(cot.at[:, cols], cot_out.at[:, cols])
        cot_own[:, cols] = dot_nn(own, piece).astype(BF)
        downs.wait(at)
        for half in range(2):
            term = dot_nt(piece, wd[half, :, cols])
            total[half] = term if at == 0 else total[half] + term
    for half in range(2):
        d_hidden[half] = total[half]
    stores.add(d_hidden, d_hidden_out)
    stores.finish()


def second_kernel(
    x, gain, own_target, d_hidden_in, up_a, up_b,
    gain_term, own_rows, dn, normed_out, d_act_a_out, d_act_b_out, hidden_a_out, hidden_b_out,
    wu, su, normed, d_act, hidden, d_hidden, sh, so,
):
    ups = Weights((up_a, up_b), wu, su)
    ups.start_all()
    fetch = pltpu.make_async_copy(d_hidden_in, d_hidden, sh)
    fetch.start()
    stores = Stores(so)
    scale = row_scale(x)
    total = normed_times_up(x, scale, gain, normed, normed_out, stores, ups, wu)
    fetch.wait()
    for half in range(2):
        value, slope = silu_parts(total[half])
        hidden[half] = value.astype(BF)
        d_act[half] = (d_hidden[half] * slope).astype(BF)
    stores.add(d_act.at[0], d_act_a_out)
    stores.add(d_act.at[1], d_act_b_out)
    stores.add(hidden.at[0], hidden_a_out)
    stores.add(hidden.at[1], hidden_b_out)
    own = one_hot(own_target[...], TALL)
    for cols in chunks(x.shape[1]):
        term = dot_nn(d_act[0], wu[0, :, cols]) + dot_nn(d_act[1], wu[1, :, cols])
        dn[:, cols] = term.astype(BF)
        gain_term[:, cols] = jnp.sum(term * normed[:, cols].astype(F32), axis=0, keepdims=True) / gain[:, cols]
        own_rows[:, cols] = dot_nn(own, x[:, cols]).astype(BF)
    stores.finish()


def target_kernel(
    to_target, hidden_a, hidden_b, down_a, down_b, near_out, far_out, wd, sd, proj, hidden, sh, so
):
    fetches = [pltpu.make_async_copy(ref, hidden.at[at], sh.at[at]) for at, ref in enumerate((hidden_a, hidden_b))]
    for fetch in fetches:
        fetch.start()
    downs = Weights((down_a, down_b), wd, sd)
    downs.start_all()
    stores = Stores(so)
    sort = one_hot(to_target[...], TALL)
    left = []
    for half, fetch in enumerate(fetches):
        fetch.wait()
        left.append(dot_nn(sort, hidden[half]).astype(BF))
    for at, cols in enumerate(chunks(proj.shape[1])):
        downs.wait(at)
        proj[:, cols] = (dot_nn(left[0], wd[0, :, cols]) + dot_nn(left[1], wd[1, :, cols])).astype(BF)
        stores.add(proj.at[: 4 * ROWS, cols], near_out.at[:, cols])
        stores.add(proj.at[4 * ROWS :, cols], far_out.at[:, cols])
    stores.finish()


def sum_kernel(near, far, mine, second, third, fourth):
    for cols in chunks(near.shape[1]):
        total = near[:, cols].astype(F32) + far[:, cols].astype(F32)
        mine[:, cols] = total[:ROWS]
        for at, out in enumerate((second, third, fourth)):
            out[:, cols] = total[(at + 1) * ROWS : (at + 2) * ROWS].astype(BF)


def second_out_kernel(own_rows, mine, second, third, fourth, out):
    for cols in chunks(out.shape[1]):
        total = mine[:, cols] + second[:, cols].astype(F32) + third[:, cols].astype(F32) + fourth[:, cols].astype(F32)
        out[:, cols] = (own_rows[:, cols].astype(F32) + total).astype(BF)


def first_back_kernel(
    c, gain, gain_two, slope_in, normed_in, d_act_two_b, hidden_one_b, hidden_two_b, up_a, up_b, down_a, down_b,
    dn, c_out, d_act_a_out, thin_out,
    wu, wd, su, sd, d_act, slope, normed, thin, sh, so,
):
    width = c.shape[1]
    downs = Weights((down_a, down_b), wd, sd)
    ups = Weights((up_a, up_b), wu, su)
    downs.start_all()
    fetches = [pltpu.make_async_copy(slope_in, slope, sh.at[0]), pltpu.make_async_copy(normed_in, normed, sh.at[1])]
    for at, source in enumerate((d_act_two_b, hidden_one_b, hidden_two_b)):
        fetches.append(pltpu.make_async_copy(source, thin.at[at], sh.at[2 + at]))
    stores = Stores(so)
    stores.add(c, c_out)
    total = [None, None]
    for at, cols in enumerate(chunks(width)):
        downs.wait(at)
        if at == 0:
            for fetch in fetches:
                fetch.start()
        ups.start(at)
        for half in range(2):
            term = dot_nt(c[:, cols], wd[half, :, cols])
            total[half] = term if at == 0 else total[half] + term
    for fetch in fetches:
        fetch.wait()
    for half in range(2):
        d_act[half] = (total[half] * slope[half]).astype(BF)
    stores.add(d_act.at[0], d_act_a_out)
    stores.add(d_act.at[1], thin_out.at[0])
    stores.add(thin, thin_out.at[1:4])
    gain_pieces = []
    for at, cols in enumerate(chunks(width)):
        ups.wait(at)
        term = dot_nn(d_act[0], wu[0, :, cols]) + dot_nn(d_act[1], wu[1, :, cols])
        dn[:, cols] = term.astype(BF)
        product = jnp.sum(term * normed[:, cols].astype(F32), axis=0, keepdims=True)
        gain_pieces.append(product / gain[:, cols] + gain_two[:, cols])
    line = jnp.concatenate(gain_pieces, axis=1)
    lanes = width // 8
    grid = jnp.concatenate([line[:, lanes * at : lanes * (at + 1)] for at in range(8)], axis=0)
    high = grid.astype(BF).astype(F32)
    both = jnp.concatenate([high, grid - high], axis=0).astype(BF)
    for block in range(CHIPS):
        dn[block * ROWS : (block + 1) * ROWS, width:] = both
    stores.finish()


def add_blocks(blocks, cols):
    total = blocks[0:ROWS, cols].astype(F32)
    for at in range(ROWS, blocks.shape[0], ROWS):
        total = total + blocks[at : at + ROWS, cols].astype(F32)
    return total


def add_kernel(blocks, x, out):
    for cols in chunks(x.shape[1]):
        out[:, cols] = (x[:, cols].astype(F32) + add_blocks(blocks, cols)).astype(BF)


def rows_back_kernel(blocks, x, c, gain, out, spread):
    width = x.shape[1]
    scale = row_scale(x)
    along = jnp.zeros((ROWS, 128), F32)
    for cols in chunks(width):
        piece = add_blocks(blocks, cols) * gain[:, cols]
        spread[:, cols] = piece
        product = piece * (x[:, cols].astype(F32) * scale)
        for at in range(0, CHUNK, 128):
            along = along + product[:, at : at + 128]
    mean = jnp.sum(along, axis=-1, keepdims=True) * (1.0 / width)
    for cols in chunks(width):
        vhat = x[:, cols].astype(F32) * scale
        out[:, cols] = (c[:, cols].astype(F32) + scale * (spread[:, cols] - vhat * mean)).astype(BF)


def last_kernel(blocks, x, c, gain, out, gain_sum, spread):
    width = x.shape[1]
    rows_back_kernel(blocks, x, c, gain, out, spread)
    extra = add_blocks(blocks, slice(width, blocks.shape[1]))
    line = extra[:8] + extra[8:]
    gain_sum[...] = jnp.concatenate([line[at : at + 1] for at in range(8)], axis=1)


def grads_kernel(*refs):
    normed, c, (d_act_one, d_act_two, hidden_one, hidden_two, other) = refs[0:4], refs[4:8], refs[8:13]
    out_up, out_down, left_up, left_down = refs[13:17]

    @pl.when(pl.program_id(0) == 0)
    def _():
        for at, own in enumerate((d_act_one, d_act_two)):
            left_up[:, 2 * at * TALL : (2 * at + 1) * TALL] = own[...].T
            left_up[:, (2 * at + 1) * TALL : (2 * at + 2) * TALL] = other[at].T
        for at, own in enumerate((hidden_one, hidden_two)):
            left_down[:, 2 * at * TALL : (2 * at + 1) * TALL] = own[...].T
            left_down[:, (2 * at + 1) * TALL : (2 * at + 2) * TALL] = other[2 + at].T

    right = jnp.concatenate([ref[...] for ref in normed], axis=0)
    out_up[...] = dot_nn(left_up[...], right).astype(BF)
    right = jnp.concatenate([ref[...] for ref in c], axis=0)
    out_down[...] = dot_nn(left_down[...], right).astype(BF)


def in_vmem(*dims, dtype=BF):
    return pltpu.VMEM(dims, dtype)


def shape(*dims, dtype=BF):
    return jax.ShapeDtypeStruct(dims, dtype)


def in_hbm(value):
    return pltpu.with_memory_space_constraint(value, pltpu.HBM)


def call(kernel, outs, args, from_hbm=(), hbm_outs=(), scratch=(), limit=16, flops=0, moved=0):
    return pl.pallas_call(
        kernel,
        out_shape=list(outs) + [pltpu.HBM(out.shape, out.dtype) for out in hbm_outs],
        in_specs=[VM] * len(args) + [HBM] * len(from_hbm),
        out_specs=[VM] * len(outs) + [HBM] * len(hbm_outs),
        scratch_shapes=scratch,
        compiler_params=pltpu.CompilerParams(vmem_limit_bytes=limit * VMEM_MB),
        cost_estimate=pl.CostEstimate(flops=flops, bytes_accessed=moved, transcendentals=0),
    )(*args, *[in_hbm(value) for value in from_hbm])


def kept(*dims, dtype=BF):
    return pltpu.VMEM(dims, dtype)


def dma(*dims):
    return pltpu.SemaphoreType.DMA(dims)


def weight_scratch(units, width, count):
    return [kept(2, units, width)] * count + [dma(width // CHUNK, 2)] * count


def to_chips(blocks):
    return lax.all_to_all(
        blocks, "peer", split_axis=0, concat_axis=0, tiled=True, axis_index_groups=SAME_CORE
    )


def spread(rows):
    width = rows.shape[1]
    return call(spread_kernel, [in_vmem(TALL, width)], [rows], limit=4, moved=TALL * width * 4)[0]


def from_chips(rows):
    return to_chips(spread(rows))


def swap(value):
    return lax.ppermute(value, "peer", SIBLING)


def after(value, *earlier):
    return lax.optimization_barrier((value,) + earlier)[0]


def together(*values):
    return lax.optimization_barrier(values)


def passed_along(value, steps):
    count = lax.axis_size("section")
    leading, last = (max(0, -steps), min(count, count - steps))
    return lax.ppermute(value, "section", [(source, source + steps) for source in range(leading, last)])


def local(acts, cotangent, gain, w_up, w_down, matching):
    section = lax.axis_index("section")
    peer = lax.axis_index("peer")
    core = peer % 2
    chip = peer // 2
    rows_in, cot_in, up, down = acts[0], cotangent[0], w_up[0], w_down[0]
    units, width = up.shape
    flops = 4 * TALL * units * width
    moved = 2 * TALL * width * 2
    steps = width // CHUNK
    tall, block, slim = shape(TALL, width), shape(ROWS, width), shape(TALL, units)
    pair_f32 = shape(2, TALL, units, dtype=F32)

    cot_b = swap(cot_in)
    up_b, down_b = swap(after(up, cot_b)), swap(after(down, cot_b))

    before = lax.dynamic_index_in_dim(matching, jnp.maximum(section - 1, 0), 0, keepdims=False)
    mine = jnp.where(core == 0, before[0::2], before[1::2])
    chips = jnp.arange(CHIPS, dtype=jnp.int32)
    slots = jnp.arange(ROWS, dtype=jnp.int32)
    pair = jnp.arange(2, dtype=jnp.int32)
    wanted = slots[None, :] ^ mine[:, None]
    apart_y, apart_z = (wanted // 2 - chip) % 4, (wanted // 8) ^ (chip // 4)
    pick = ((apart_z * 4 + apart_y) * ROWS + (wanted % 2) * CHIPS + chips[:, None]).reshape(TALL, 1)
    cot_index = (jnp.where(pair == core, 0, ROWS)[:, None] + 2 * chips[None, :] + core).reshape(ROWS, 1)
    owner = ((chip // 4) ^ pair)[:, None] * 4 + ((chip + jnp.arange(4, dtype=jnp.int32)) % 4)[None, :]
    to_target = (owner.reshape(CHIPS, 1, 1) * 2 + pair[None, :, None]) ^ mine[None, None, :]
    to_target = (to_target + chips[None, None, :] * ROWS).reshape(TALL, 1)
    own_target = to_target[:ROWS]
    own_pick = (chip * ROWS + slots).reshape(ROWS, 1)
    out_index = (jnp.where(slots % 2 == core, 0, ROWS) + core * CHIPS + slots // 2).reshape(ROWS, 1)

    wide_rows, cot_half = call(
        prepare_kernel, [in_vmem(TALL, width), block], [cot_b, cot_index], [rows_in, cot_in], [],
        [kept(ROWS, width), pltpu.SemaphoreType.DMA, dma(CHIPS)], limit=8, moved=moved,
    )
    even = lax.ppermute(cot_half, "peer", ALONG_Y[3][0::2])
    wide_rows, even = together(wide_rows, even)
    x_one = to_chips(wide_rows)
    rest = after(cot_half, even)
    cot_y = [lax.ppermute(rest, "peer", pairs) for pairs in (ALONG_Y[3][1::2], ALONG_Y[2], ALONG_Y[1])]
    cot_a, cot_b = call(join_kernel, [shape(2 * ROWS, width)] * 2, [cot_half, even] + cot_y, moved=moved)
    x_one, cot_a, cot_b = together(x_one, cot_a, cot_b)
    cot_za = lax.ppermute(cot_a, "peer", ACROSS_Z)
    proj, normed_one, slope_one, hidden_one, hidden_one_b = call(
        forward_kernel, [in_vmem(TALL, width)], [x_one, gain], [up, up_b, down, down_b], [tall, pair_f32, slim, slim],
        weight_scratch(units, width, 2)
        + [kept(TALL, width), kept(2, TALL, units, dtype=F32), kept(2, TALL, units), dma(steps + 3)],
        limit=36, flops=3 * flops, moved=6 * moved,
    )
    proj, cot_za = together(proj, cot_za)
    blocks = to_chips(proj)
    first = call(add_kernel, [block], [blocks, rows_in], moved=moved)[0]
    arrived = passed_along(first, 1)
    cot_zb = lax.ppermute(after(cot_b, first), "peer", ACROSS_Z)
    arrived, cot_zb = together(arrived, cot_zb)
    cot_all = [cot_a, cot_b, cot_za, cot_zb]
    x_two = from_chips(arrived)
    cot_own, cot, d_hidden = call(
        cot_kernel, [block], cot_all + [pick, own_pick], [down, down_b], [tall, pair_f32],
        weight_scratch(units, width, 1) + [kept(TALL, width), kept(2, TALL, units, dtype=F32), dma(steps + 1)],
        limit=20, flops=3 * flops, moved=3 * moved,
    )
    gain_two, own_rows, d_normed, normed_two, d_act_two, d_act_two_b, hidden_two, hidden_two_b = call(
        second_kernel, [shape(1, width, dtype=F32), block, in_vmem(TALL, width)],
        [x_two, gain, own_target], [d_hidden, up, up_b], [tall, slim, slim, slim, slim],
        weight_scratch(units, width, 1)
        + [kept(TALL, width), kept(2, TALL, units), kept(2, TALL, units), kept(2, TALL, units, dtype=F32),
           pltpu.SemaphoreType.DMA, dma(steps + 4)],
        limit=28, flops=3 * flops, moved=4 * moved,
    )
    blocks = to_chips(d_normed)
    parts = call(
        target_kernel, [], [to_target], [hidden_two, hidden_two_b, down, down_b],
        [shape(4 * ROWS, width)] * 2,
        weight_scratch(units, width, 1) + [kept(TALL, width), kept(2, TALL, units), dma(2), dma(2 * steps)],
        limit=20, flops=2 * flops, moved=3 * moved,
    )
    blocks = after(blocks, *parts)
    d_two = call(
        rows_back_kernel, [block], [blocks, arrived, cot_own, gain], scratch=[kept(ROWS, width, dtype=F32)], moved=moved
    )[0]
    landed = passed_along(d_two, -1)
    c_all = from_chips(landed)
    near, far, c_all = together(*parts, c_all)
    far = lax.ppermute(far, "peer", ACROSS_Z)
    d_normed, c_one, d_act_one, thin = call(
        first_back_kernel, [in_vmem(TALL, width + width // 8)], [c_all, gain, gain_two],
        [slope_one, normed_one, d_act_two_b, hidden_one_b, hidden_two_b, up, up_b, down, down_b],
        [tall, slim, shape(4, TALL, units)],
        weight_scratch(units, width, 2)
        + [kept(2, TALL, units), kept(2, TALL, units, dtype=F32), kept(TALL, width), kept(3, TALL, units), dma(5), dma(4)],
        limit=36, flops=3 * flops, moved=6 * moved,
    )
    ready = d_normed
    d_normed, far = together(d_normed, far)
    blocks = to_chips(d_normed)
    sums = call(sum_kernel, [shape(ROWS, width, dtype=F32), block, block, block], [near, far], moved=moved)
    sums = [sums[0]] + [lax.ppermute(sums[apart], "peer", ALONG_Y[apart]) for apart in (1, 2, 3)]
    wide = []
    for value in (normed_one, normed_two, c_one, cot):
        wide += [value, swap(after(value, ready))]
    slims = [d_act_one, d_act_two, hidden_one, hidden_two, swap(thin)]
    step = 2560
    grad_up, grad_down = pl.pallas_call(
        grads_kernel,
        grid=(width // step,),
        out_shape=[shape(units, width)] * 2,
        in_specs=[pl.BlockSpec((TALL, step), lambda i: (0, i))] * 8
        + [pl.BlockSpec((TALL, units), lambda i: (0, 0))] * 4
        + [pl.BlockSpec((4, TALL, units), lambda i: (0, 0, 0))],
        out_specs=[pl.BlockSpec((units, step), lambda i: (0, i))] * 2,
        scratch_shapes=[kept(units, 4 * TALL)] * 2,
        compiler_params=pltpu.CompilerParams(vmem_limit_bytes=40 * VMEM_MB),
        cost_estimate=pl.CostEstimate(flops=4 * flops, bytes_accessed=8 * moved, transcendentals=0),
    )(*[in_hbm(value) for value in wide], *[in_hbm(value) for value in slims])

    d_one, gain_sum = call(
        last_kernel, [block, shape(1, width, dtype=F32)], [after(blocks, grad_up), rows_in, landed, gain],
        scratch=[kept(ROWS, width, dtype=F32)], moved=moved,
    )
    second = call(second_out_kernel, [block], [after(own_rows, grad_up)] + sums, moved=moved // 4)[0]
    second = call(pick_kernel, [block], [second, swap(second), out_index])[0]
    grad_gain = gain_sum + swap(gain_sum)
    return (d_one[None], second[None], grad_up[None], grad_down[None], grad_gain)


def solution(mesh):
    wide = P("section", "peer", None)
    in_specs = (wide, wide, P("section", None), wide, wide, P())
    out_specs = (wide, wide, wide, wide, P("section", None))
    return jax.shard_map(local, mesh=mesh, in_specs=in_specs, out_specs=out_specs, check_vma=False)
```

```python
import jax
import jax.numpy as jnp
from jax import lax
from jax.experimental import pallas as pl
from jax.experimental.pallas import tpu as pltpu
from jax.sharding import PartitionSpec as P

BF = jnp.bfloat16
F32 = jnp.float32
ROWS = 16
CHIPS = 8
TALL = CHIPS * ROWS
CHUNK = 1024
VMEM_MB = 1024 * 1024

SAME_CORE = [[2 * chip + core for chip in range(CHIPS)] for core in range(2)]
SIBLING = [(peer, peer ^ 1) for peer in range(16)]
ACROSS_Z = [(peer, peer ^ 8) for peer in range(16)]
ALONG_Y = [[(peer, peer // 8 * 8 + (peer + 2 * apart) % 8) for peer in range(16)] for apart in range(4)]

VM = pl.BlockSpec(memory_space=pltpu.VMEM)
HBM = pl.BlockSpec(memory_space=pltpu.HBM)


def dot_nt(left, right):
    return lax.dot_general(left, right, (((1,), (1,)), ((), ())), preferred_element_type=F32)


def dot_nn(left, right):
    return jnp.dot(left, right, preferred_element_type=F32)


def chunks(width):
    return [slice(at, at + CHUNK) for at in range(0, width, CHUNK)]


def row_scale(x_ref):
    rows, width = x_ref.shape
    total = jnp.zeros((rows, 128), F32)
    for at in range(0, width, 128):
        piece = x_ref[:, at : at + 128].astype(F32)
        total = total + piece * piece
    mean = jnp.sum(total, axis=-1, keepdims=True) * (1.0 / width)
    return lax.rsqrt(mean + 1e-05)


def silu_parts(act):
    sigma = jax.nn.sigmoid(act)
    return act * sigma, sigma * (1.0 + act * (1.0 - sigma))


def one_hot(index, width):
    lanes = lax.broadcasted_iota(jnp.int32, (index.shape[0], width), 1)
    return jnp.where(lanes == index, 1.0, 0.0).astype(BF)


class Weights:
    def __init__(self, sources, buffer, sems):
        self.copies = []
        for at, cols in enumerate(chunks(sources[0].shape[1])):
            self.copies.append(
                [
                    pltpu.make_async_copy(source.at[:, cols], buffer.at[which, :, cols], sems.at[at, which])
                    for which, source in enumerate(sources)
                ]
            )

    def start(self, at):
        for copy in self.copies[at]:
            copy.start()

    def start_all(self):
        for at in range(len(self.copies)):
            self.start(at)

    def wait(self, at):
        for copy in self.copies[at]:
            copy.wait()


class Stores:
    def __init__(self, sems):
        self.sems = sems
        self.copies = []

    def add(self, source, target):
        copy = pltpu.make_async_copy(source, target, self.sems.at[len(self.copies)])
        copy.start()
        self.copies.append(copy)

    def finish(self):
        for copy in self.copies:
            copy.wait()


def normed_times_up(x, scale, gain, normed, normed_out, stores, ups, wu, following=None):
    total = [None, None]
    for at, cols in enumerate(chunks(x.shape[1])):
        piece = (x[:, cols].astype(F32) * scale * gain[:, cols]).astype(BF)
        normed[:, cols] = piece
        stores.add(normed.at[:, cols], normed_out.at[:, cols])
        ups.wait(at)
        if following is not None:
            following.start(at)
        for half in range(2):
            term = dot_nt(piece, wu[half, :, cols])
            total[half] = term if at == 0 else total[half] + term
    return total


def forward_kernel(
    x, gain, up_a, up_b, down_a, down_b,
    proj_out, normed_out, slope_out, hidden_a_out, hidden_b_out,
    wu, wd, su, sd, proj, normed, slope, hidden, so,
):
    ups = Weights((up_a, up_b), wu, su)
    downs = Weights((down_a, down_b), wd, sd)
    ups.start_all()
    stores = Stores(so)
    scale = row_scale(x)
    total = normed_times_up(x, scale, gain, normed, normed_out, stores, ups, wu, downs)
    for half in range(2):
        value, slant = silu_parts(total[half])
        slope[half] = slant
        hidden[half] = value.astype(BF)
    stores.add(slope, slope_out)
    stores.add(hidden.at[0], hidden_a_out)
    stores.add(hidden.at[1], hidden_b_out)
    for at, cols in enumerate(chunks(x.shape[1])):
        downs.wait(at)
        proj[:, cols] = (dot_nn(hidden[0], wd[0, :, cols]) + dot_nn(hidden[1], wd[1, :, cols])).astype(BF)
        stores.add(proj.at[:, cols], proj_out.at[:, cols])
    stores.finish()


def pick_kernel(*refs):
    sources, index, out = refs[:-2], refs[-2], refs[-1]
    choose = one_hot(index[...], len(sources) * ROWS)
    for cols in chunks(out.shape[1]):
        rows = jnp.concatenate([source[:, cols] for source in sources], axis=0)
        out[:, cols] = dot_nn(choose, rows).astype(BF)


def join_kernel(fourth, third, odd, even, own, first_pair, second_pair):
    first_pair[:ROWS, :] = own[...]
    first_pair[ROWS:, :] = even[...] + odd[...]
    second_pair[:ROWS, :] = third[...]
    second_pair[ROWS:, :] = fourth[...]


def finish_kernel(own, other, index, gain_own, gain_other, out, gain_out):
    pick_kernel(own, other, index, out)
    gain_out[...] = gain_own[...] + gain_other[...]


def prepare_kernel(other, index, rows_in, own_in, wide, share, held, sems):
    copies = [pltpu.make_async_copy(ref, held.at[at], sems.at[at]) for at, ref in enumerate((rows_in, own_in))]
    for copy in copies:
        copy.start()
    for copy in copies:
        copy.wait()
    pick_kernel(held.at[1], other, index, share)
    spread_kernel(held.at[0], wide)


def spread_kernel(rows, out):
    for at in range(0, out.shape[0], ROWS):
        out[at : at + ROWS, :] = rows[...]


def cot_kernel(*refs):
    sources, (pick, own_pick, down_a, down_b) = refs[:4], refs[4:8]
    cot_own, cot_out, d_hidden_out, wd, sd, cot, d_hidden, so = refs[8:]
    downs = Weights((down_a, down_b), wd, sd)
    downs.start_all()
    stores = Stores(so)
    choose = one_hot(pick[...], TALL)
    own = one_hot(own_pick[...], TALL)
    total = [None, None]
    for at, cols in enumerate(chunks(cot.shape[1])):
        rows = jnp.concatenate([source[:, cols] for source in sources], axis=0)
        piece = dot_nn(choose, rows).astype(BF)
        cot[:, cols] = piece
        stores.add(cot.at[:, cols], cot_out.at[:, cols])
        cot_own[:, cols] = dot_nn(own, piece).astype(BF)
        downs.wait(at)
        for half in range(2):
            term = dot_nt(piece, wd[half, :, cols])
            total[half] = term if at == 0 else total[half] + term
    for half in range(2):
        d_hidden[half] = total[half]
    stores.add(d_hidden, d_hidden_out)
    stores.finish()


def second_kernel(
    x, gain, own_target, d_hidden_in, up_a, up_b,
    gain_term, own_rows_out, dn_out, normed_out, d_act_a_out, d_act_b_out, hidden_a_out, hidden_b_out,
    wu, su, own_rows, dn, normed, d_act, hidden, d_hidden, sh, so,
):
    ups = Weights((up_a, up_b), wu, su)
    ups.start_all()
    fetch = pltpu.make_async_copy(d_hidden_in, d_hidden, sh)
    fetch.start()
    stores = Stores(so)
    scale = row_scale(x)
    total = normed_times_up(x, scale, gain, normed, normed_out, stores, ups, wu)
    fetch.wait()
    for half in range(2):
        value, slope = silu_parts(total[half])
        hidden[half] = value.astype(BF)
        d_act[half] = (d_hidden[half] * slope).astype(BF)
    stores.add(d_act.at[0], d_act_a_out)
    stores.add(d_act.at[1], d_act_b_out)
    stores.add(hidden.at[0], hidden_a_out)
    stores.add(hidden.at[1], hidden_b_out)
    own = one_hot(own_target[...], TALL)
    for cols in chunks(x.shape[1]):
        own_rows[:, cols] = dot_nn(own, x[:, cols]).astype(BF)
    stores.add(own_rows, own_rows_out)
    for cols in chunks(x.shape[1]):
        term = dot_nn(d_act[0], wu[0, :, cols]) + dot_nn(d_act[1], wu[1, :, cols])
        dn[:, cols] = term.astype(BF)
        stores.add(dn.at[:, cols], dn_out.at[:, cols])
        gain_term[:, cols] = jnp.sum(term * normed[:, cols].astype(F32), axis=0, keepdims=True) / gain[:, cols]
    stores.finish()


def target_kernel(
    to_target, hidden_a, hidden_b, down_a, down_b, near_out, far_out, wd, sd, proj, hidden, sh, so
):
    fetches = [pltpu.make_async_copy(ref, hidden.at[at], sh.at[at]) for at, ref in enumerate((hidden_a, hidden_b))]
    for fetch in fetches:
        fetch.start()
    downs = Weights((down_a, down_b), wd, sd)
    downs.start_all()
    stores = Stores(so)
    sort = one_hot(to_target[...], TALL)
    left = []
    for half, fetch in enumerate(fetches):
        fetch.wait()
        left.append(dot_nn(sort, hidden[half]).astype(BF))
    for at, cols in enumerate(chunks(proj.shape[1])):
        downs.wait(at)
        proj[:, cols] = (dot_nn(left[0], wd[0, :, cols]) + dot_nn(left[1], wd[1, :, cols])).astype(BF)
        stores.add(proj.at[: 4 * ROWS, cols], near_out.at[:, cols])
        stores.add(proj.at[4 * ROWS :, cols], far_out.at[:, cols])
    stores.finish()


def sum_kernel(near, far, mine, second, third, fourth):
    for cols in chunks(near.shape[1]):
        total = near[:, cols].astype(F32) + far[:, cols].astype(F32)
        mine[:, cols] = total[:ROWS]
        for at, out in enumerate((second, third, fourth)):
            out[:, cols] = total[(at + 1) * ROWS : (at + 2) * ROWS].astype(BF)


def second_out_kernel(own_rows, mine, second, third, fourth, out):
    for cols in chunks(out.shape[1]):
        total = mine[:, cols] + second[:, cols].astype(F32) + third[:, cols].astype(F32) + fourth[:, cols].astype(F32)
        out[:, cols] = (own_rows[:, cols].astype(F32) + total).astype(BF)


def first_back_kernel(
    c, gain, gain_two, slope_in, normed_in, d_act_two_b, hidden_one_b, hidden_two_b, up_a, up_b, down_a, down_b,
    dn_out, c_out, d_act_a_out, thin_out,
    wu, wd, su, sd, dn, d_act, slope, normed, thin, sh, so,
):
    width = c.shape[1]
    downs = Weights((down_a, down_b), wd, sd)
    ups = Weights((up_a, up_b), wu, su)
    downs.start_all()
    fetches = [pltpu.make_async_copy(slope_in, slope, sh.at[0]), pltpu.make_async_copy(normed_in, normed, sh.at[1])]
    for at, source in enumerate((d_act_two_b, hidden_one_b, hidden_two_b)):
        fetches.append(pltpu.make_async_copy(source, thin.at[at], sh.at[2 + at]))
    stores = Stores(so)
    stores.add(c, c_out)
    total = [None, None]
    for at, cols in enumerate(chunks(width)):
        downs.wait(at)
        if at == 0:
            for fetch in fetches:
                fetch.start()
        ups.start(at)
        for half in range(2):
            term = dot_nt(c[:, cols], wd[half, :, cols])
            total[half] = term if at == 0 else total[half] + term
    for fetch in fetches:
        fetch.wait()
    for half in range(2):
        d_act[half] = (total[half] * slope[half]).astype(BF)
    stores.add(d_act.at[0], d_act_a_out)
    stores.add(d_act.at[1], thin_out.at[0])
    stores.add(thin, thin_out.at[1:4])
    gain_pieces = []
    for at, cols in enumerate(chunks(width)):
        ups.wait(at)
        term = dot_nn(d_act[0], wu[0, :, cols]) + dot_nn(d_act[1], wu[1, :, cols])
        dn[:, cols] = term.astype(BF)
        stores.add(dn.at[:, cols], dn_out.at[:, cols])
        product = jnp.sum(term * normed[:, cols].astype(F32), axis=0, keepdims=True)
        gain_pieces.append(product / gain[:, cols] + gain_two[:, cols])
    line = jnp.concatenate(gain_pieces, axis=1)
    lanes = width // 8
    grid = jnp.concatenate([line[:, lanes * at : lanes * (at + 1)] for at in range(8)], axis=0)
    high = grid.astype(BF).astype(F32)
    both = jnp.concatenate([high, grid - high], axis=0).astype(BF)
    for block in range(CHIPS):
        dn[block * ROWS : (block + 1) * ROWS, width:] = both
    stores.add(dn.at[:, width:], dn_out.at[:, width:])
    stores.finish()


def add_blocks(blocks, cols):
    total = blocks[0:ROWS, cols].astype(F32)
    for at in range(ROWS, blocks.shape[0], ROWS):
        total = total + blocks[at : at + ROWS, cols].astype(F32)
    return total


def add_kernel(blocks, x, out):
    for cols in chunks(x.shape[1]):
        out[:, cols] = (x[:, cols].astype(F32) + add_blocks(blocks, cols)).astype(BF)


def rows_back_kernel(blocks, x, c, gain, out, spread):
    width = x.shape[1]
    scale = row_scale(x)
    along = jnp.zeros((ROWS, 128), F32)
    for cols in chunks(width):
        piece = add_blocks(blocks, cols) * gain[:, cols]
        spread[:, cols] = piece
        product = piece * (x[:, cols].astype(F32) * scale)
        for at in range(0, CHUNK, 128):
            along = along + product[:, at : at + 128]
    mean = jnp.sum(along, axis=-1, keepdims=True) * (1.0 / width)
    for cols in chunks(width):
        vhat = x[:, cols].astype(F32) * scale
        out[:, cols] = (c[:, cols].astype(F32) + scale * (spread[:, cols] - vhat * mean)).astype(BF)


def last_kernel(blocks, x, c, gain, out, gain_sum, spread):
    width = x.shape[1]
    rows_back_kernel(blocks, x, c, gain, out, spread)
    extra = add_blocks(blocks, slice(width, blocks.shape[1]))
    line = extra[:8] + extra[8:]
    gain_sum[...] = jnp.concatenate([line[at : at + 1] for at in range(8)], axis=1)


def grads_kernel(*refs):
    normed, c, (d_act_one, d_act_two, hidden_one, hidden_two, other) = refs[0:4], refs[4:8], refs[8:13]
    out_up, out_down, left_up, left_down = refs[13:17]

    @pl.when(pl.program_id(0) == 0)
    def _():
        for at, own in enumerate((d_act_one, d_act_two)):
            left_up[:, 2 * at * TALL : (2 * at + 1) * TALL] = own[...].T
            left_up[:, (2 * at + 1) * TALL : (2 * at + 2) * TALL] = other[at].T
        for at, own in enumerate((hidden_one, hidden_two)):
            left_down[:, 2 * at * TALL : (2 * at + 1) * TALL] = own[...].T
            left_down[:, (2 * at + 1) * TALL : (2 * at + 2) * TALL] = other[2 + at].T

    right = jnp.concatenate([ref[...] for ref in normed], axis=0)
    out_up[...] = dot_nn(left_up[...], right).astype(BF)
    right = jnp.concatenate([ref[...] for ref in c], axis=0)
    out_down[...] = dot_nn(left_down[...], right).astype(BF)


def in_vmem(*dims, dtype=BF):
    return pltpu.VMEM(dims, dtype)


def shape(*dims, dtype=BF):
    return jax.ShapeDtypeStruct(dims, dtype)


def in_hbm(value):
    return pltpu.with_memory_space_constraint(value, pltpu.HBM)


def call(kernel, outs, args, from_hbm=(), hbm_outs=(), scratch=(), limit=16, flops=0, moved=0):
    return pl.pallas_call(
        kernel,
        out_shape=list(outs) + [pltpu.HBM(out.shape, out.dtype) for out in hbm_outs],
        in_specs=[VM] * len(args) + [HBM] * len(from_hbm),
        out_specs=[VM] * len(outs) + [HBM] * len(hbm_outs),
        scratch_shapes=scratch,
        compiler_params=pltpu.CompilerParams(vmem_limit_bytes=limit * VMEM_MB),
        cost_estimate=pl.CostEstimate(flops=flops, bytes_accessed=moved, transcendentals=0),
    )(*args, *[in_hbm(value) for value in from_hbm])


def kept(*dims, dtype=BF):
    return pltpu.VMEM(dims, dtype)


def dma(*dims):
    return pltpu.SemaphoreType.DMA(dims)


def weight_scratch(units, width, count):
    return [kept(2, units, width)] * count + [dma(width // CHUNK, 2)] * count


def to_chips(blocks):
    return lax.all_to_all(
        blocks, "peer", split_axis=0, concat_axis=0, tiled=True, axis_index_groups=SAME_CORE
    )


def spread(rows):
    width = rows.shape[1]
    return call(spread_kernel, [in_vmem(TALL, width)], [rows], limit=4, moved=TALL * width * 4)[0]


def from_chips(rows):
    return to_chips(spread(rows))


def swap(value):
    return lax.ppermute(value, "peer", SIBLING)


def after(value, *earlier):
    return lax.optimization_barrier((value,) + earlier)[0]


def together(*values):
    return lax.optimization_barrier(values)


def passed_along(value, steps):
    count = lax.axis_size("section")
    leading, last = (max(0, -steps), min(count, count - steps))
    return lax.ppermute(value, "section", [(source, source + steps) for source in range(leading, last)])


def local(acts, cotangent, gain, w_up, w_down, matching):
    section = lax.axis_index("section")
    peer = lax.axis_index("peer")
    core = peer % 2
    chip = peer // 2
    rows_in, cot_in, up, down = acts[0], cotangent[0], w_up[0], w_down[0]
    units, width = up.shape
    flops = 4 * TALL * units * width
    moved = 2 * TALL * width * 2
    steps = width // CHUNK
    tall, block, slim = shape(TALL, width), shape(ROWS, width), shape(TALL, units)
    pair_f32 = shape(2, TALL, units, dtype=F32)

    cot_b = swap(cot_in)
    up_b, down_b = swap(after(up, cot_b)), swap(after(down, cot_b))

    before = lax.dynamic_index_in_dim(matching, jnp.maximum(section - 1, 0), 0, keepdims=False)
    mine = jnp.where(core == 0, before[0::2], before[1::2])
    chips = jnp.arange(CHIPS, dtype=jnp.int32)
    slots = jnp.arange(ROWS, dtype=jnp.int32)
    pair = jnp.arange(2, dtype=jnp.int32)
    wanted = slots[None, :] ^ mine[:, None]
    apart_y, apart_z = (wanted // 2 - chip) % 4, (wanted // 8) ^ (chip // 4)
    pick = ((apart_z * 4 + apart_y) * ROWS + (wanted % 2) * CHIPS + chips[:, None]).reshape(TALL, 1)
    cot_index = (jnp.where(pair == core, 0, ROWS)[:, None] + 2 * chips[None, :] + core).reshape(ROWS, 1)
    owner = ((chip // 4) ^ pair)[:, None] * 4 + ((chip + jnp.arange(4, dtype=jnp.int32)) % 4)[None, :]
    to_target = (owner.reshape(CHIPS, 1, 1) * 2 + pair[None, :, None]) ^ mine[None, None, :]
    to_target = (to_target + chips[None, None, :] * ROWS).reshape(TALL, 1)
    own_target = to_target[:ROWS]
    own_pick = (chip * ROWS + slots).reshape(ROWS, 1)
    out_index = (jnp.where(slots % 2 == core, 0, ROWS) + core * CHIPS + slots // 2).reshape(ROWS, 1)

    wide_rows, cot_half = call(
        prepare_kernel, [in_vmem(TALL, width), block], [cot_b, cot_index], [rows_in, cot_in], [],
        [kept(2, ROWS, width), dma(2)], limit=8, moved=moved,
    )
    even = lax.ppermute(cot_half, "peer", ALONG_Y[3][0::2])
    wide_rows, even = together(wide_rows, even)
    x_one = to_chips(wide_rows)
    rest = after(cot_half, even)
    fourth, opposite = lax.ppermute(rest, "peer", ALONG_Y[1]), lax.ppermute(rest, "peer", ALONG_Y[2])
    odd = lax.ppermute(rest, "peer", ALONG_Y[3][1::2])
    cot_a, cot_b = call(join_kernel, [shape(2 * ROWS, width)] * 2, [fourth, opposite, odd, even, cot_half], moved=moved)
    x_one, cot_a, cot_b = together(x_one, cot_a, cot_b)
    cot_za = lax.ppermute(cot_a, "peer", ACROSS_Z)
    proj, normed_one, slope_one, hidden_one, hidden_one_b = call(
        forward_kernel, [], [x_one, gain], [up, up_b, down, down_b], [tall, tall, pair_f32, slim, slim],
        weight_scratch(units, width, 2)
        + [kept(TALL, width), kept(TALL, width), kept(2, TALL, units, dtype=F32), kept(2, TALL, units), dma(2 * steps + 3)],
        limit=36, flops=3 * flops, moved=6 * moved,
    )
    proj, cot_za = together(proj, cot_za)
    blocks = to_chips(proj)
    first = call(add_kernel, [block], [blocks, rows_in], moved=moved)[0]
    arrived = passed_along(first, 1)
    cot_zb = lax.ppermute(after(cot_b, first), "peer", ACROSS_Z)
    arrived, cot_zb = together(arrived, cot_zb)
    cot_all = [cot_a, cot_b, cot_za, cot_zb]
    x_two = from_chips(arrived)
    cot_own, cot, d_hidden = call(
        cot_kernel, [block], cot_all + [pick, own_pick], [down, down_b], [tall, pair_f32],
        weight_scratch(units, width, 1) + [kept(TALL, width), kept(2, TALL, units, dtype=F32), dma(steps + 1)],
        limit=20, flops=3 * flops, moved=3 * moved,
    )
    gain_two, own_rows, d_normed, normed_two, d_act_two, d_act_two_b, hidden_two, hidden_two_b = call(
        second_kernel, [shape(1, width, dtype=F32)],
        [x_two, gain, own_target], [d_hidden, up, up_b], [block, tall, tall, slim, slim, slim, slim],
        weight_scratch(units, width, 1)
        + [kept(ROWS, width), kept(TALL, width), kept(TALL, width), kept(2, TALL, units), kept(2, TALL, units), kept(2, TALL, units, dtype=F32),
           pltpu.SemaphoreType.DMA, dma(2 * steps + 5)],
        limit=28, flops=3 * flops, moved=4 * moved,
    )
    blocks = to_chips(d_normed)
    parts = call(
        target_kernel, [], [to_target], [hidden_two, hidden_two_b, down, down_b],
        [shape(4 * ROWS, width)] * 2,
        weight_scratch(units, width, 1) + [kept(TALL, width), kept(2, TALL, units), dma(2), dma(2 * steps)],
        limit=20, flops=2 * flops, moved=3 * moved,
    )
    blocks = after(blocks, *parts)
    d_two = call(
        rows_back_kernel, [block], [blocks, arrived, cot_own, gain], scratch=[kept(ROWS, width, dtype=F32)], moved=moved
    )[0]
    landed = passed_along(d_two, -1)
    c_all = from_chips(landed)
    near, far, c_all = together(*parts, c_all)
    far = lax.ppermute(far, "peer", ACROSS_Z)
    d_normed, c_one, d_act_one, thin = call(
        first_back_kernel, [], [c_all, gain, gain_two],
        [slope_one, normed_one, d_act_two_b, hidden_one_b, hidden_two_b, up, up_b, down, down_b],
        [shape(TALL, width + width // 8), tall, slim, shape(4, TALL, units)],
        weight_scratch(units, width, 2)
        + [kept(TALL, width + width // 8), kept(2, TALL, units), kept(2, TALL, units, dtype=F32), kept(TALL, width), kept(3, TALL, units), dma(5), dma(steps + 5)],
        limit=36, flops=3 * flops, moved=6 * moved,
    )
    ready = d_normed
    d_normed, far = together(d_normed, far)
    blocks = to_chips(d_normed)
    sums = call(sum_kernel, [shape(ROWS, width, dtype=F32), block, block, block], [near, far], moved=moved)
    sums = [sums[0]] + [lax.ppermute(sums[apart], "peer", ALONG_Y[apart]) for apart in (1, 2, 3)]
    wide = []
    for value in (normed_one, normed_two, c_one, cot):
        wide += [value, swap(after(value, ready))]
    slims = [d_act_one, d_act_two, hidden_one, hidden_two, swap(thin)]
    step = 2560
    grad_up, grad_down = pl.pallas_call(
        grads_kernel,
        grid=(width // step,),
        out_shape=[shape(units, width)] * 2,
        in_specs=[pl.BlockSpec((TALL, step), lambda i: (0, i))] * 8
        + [pl.BlockSpec((TALL, units), lambda i: (0, 0))] * 4
        + [pl.BlockSpec((4, TALL, units), lambda i: (0, 0, 0))],
        out_specs=[pl.BlockSpec((units, step), lambda i: (0, i))] * 2,
        scratch_shapes=[kept(units, 4 * TALL)] * 2,
        compiler_params=pltpu.CompilerParams(vmem_limit_bytes=40 * VMEM_MB),
        cost_estimate=pl.CostEstimate(flops=4 * flops, bytes_accessed=8 * moved, transcendentals=0),
    )(*[in_hbm(value) for value in wide], *[in_hbm(value) for value in slims])

    d_one, gain_sum = call(
        last_kernel, [block, shape(1, width, dtype=F32)], [after(blocks, grad_up), rows_in, landed, gain],
        scratch=[kept(ROWS, width, dtype=F32)], moved=moved,
    )
    second = call(second_out_kernel, [block], [after(own_rows, d_one)] + sums, moved=moved // 4)[0]
    second, grad_gain = call(
        finish_kernel, [block, shape(1, width, dtype=F32)],
        [second, swap(second), out_index, gain_sum, swap(gain_sum)],
    )
    return (d_one[None], second[None], grad_up[None], grad_down[None], grad_gain)


def solution(mesh):
    wide = P("section", "peer", None)
    in_specs = (wide, wide, P("section", None), wide, wide, P())
    out_specs = (wide, wide, wide, wide, P("section", None))
    return jax.shard_map(local, mesh=mesh, in_specs=in_specs, out_specs=out_specs, check_vma=False)
```

```python
import jax
import jax.numpy as jnp
from jax import lax
from jax.experimental import pallas as pl
from jax.experimental.pallas import tpu as pltpu
from jax.sharding import PartitionSpec as P

BF = jnp.bfloat16
F32 = jnp.float32
ROWS = 16
CHIPS = 8
TALL = CHIPS * ROWS
CHUNK = 1024
VMEM_MB = 1024 * 1024

SAME_CORE = [[2 * chip + core for chip in range(CHIPS)] for core in range(2)]
SIBLING = [(peer, peer ^ 1) for peer in range(16)]
ACROSS_Z = [(peer, peer ^ 8) for peer in range(16)]
ALONG_Y = [[(peer, peer // 8 * 8 + (peer + 2 * apart) % 8) for peer in range(16)] for apart in range(4)]

VM = pl.BlockSpec(memory_space=pltpu.VMEM)
HBM = pl.BlockSpec(memory_space=pltpu.HBM)


def dot_nt(left, right):
    return lax.dot_general(left, right, (((1,), (1,)), ((), ())), preferred_element_type=F32)


def dot_nn(left, right):
    return jnp.dot(left, right, preferred_element_type=F32)


def chunks(width):
    return [slice(at, at + CHUNK) for at in range(0, width, CHUNK)]


def row_scale(x_ref):
    rows, width = x_ref.shape
    total = jnp.zeros((rows, 128), F32)
    for at in range(0, width, 128):
        piece = x_ref[:, at : at + 128].astype(F32)
        total = total + piece * piece
    mean = jnp.sum(total, axis=-1, keepdims=True) * (1.0 / width)
    return lax.rsqrt(mean + 1e-05)


def silu_parts(act):
    sigma = jax.nn.sigmoid(act)
    return act * sigma, sigma * (1.0 + act * (1.0 - sigma))


def one_hot(index, width):
    lanes = lax.broadcasted_iota(jnp.int32, (index.shape[0], width), 1)
    return jnp.where(lanes == index, 1.0, 0.0).astype(BF)


class Weights:
    def __init__(self, sources, buffer, sems):
        self.copies = []
        for at, cols in enumerate(chunks(sources[0].shape[1])):
            self.copies.append(
                [
                    pltpu.make_async_copy(source.at[:, cols], buffer.at[which, :, cols], sems.at[at, which])
                    for which, source in enumerate(sources)
                ]
            )

    def start(self, at):
        for copy in self.copies[at]:
            copy.start()

    def start_all(self):
        for at in range(len(self.copies)):
            self.start(at)

    def wait(self, at):
        for copy in self.copies[at]:
            copy.wait()


class Stores:
    def __init__(self, sems):
        self.sems = sems
        self.copies = []

    def add(self, source, target):
        copy = pltpu.make_async_copy(source, target, self.sems.at[len(self.copies)])
        copy.start()
        self.copies.append(copy)

    def finish(self):
        for copy in self.copies:
            copy.wait()


def normed_times_up(x, scale, gain, normed, normed_out, stores, ups, wu, following=None):
    total = [None, None]
    for at, cols in enumerate(chunks(x.shape[1])):
        piece = (x[:, cols].astype(F32) * scale * gain[:, cols]).astype(BF)
        normed[:, cols] = piece
        stores.add(normed.at[:, cols], normed_out.at[:, cols])
        ups.wait(at)
        if following is not None:
            following.start(at)
        for half in range(2):
            term = dot_nt(piece, wu[half, :, cols])
            total[half] = term if at == 0 else total[half] + term
    return total


def forward_kernel(
    x, gain, up_a, up_b, down_a, down_b,
    proj_out, normed_out, slope_out, hidden_a_out, hidden_b_out,
    wu, wd, su, sd, proj, normed, slope, hidden, so,
):
    ups = Weights((up_a, up_b), wu, su)
    downs = Weights((down_a, down_b), wd, sd)
    ups.start_all()
    stores = Stores(so)
    scale = row_scale(x)
    total = normed_times_up(x, scale, gain, normed, normed_out, stores, ups, wu, downs)
    for half in range(2):
        value, slant = silu_parts(total[half])
        slope[half] = slant.astype(BF)
        hidden[half] = value.astype(BF)
    stores.add(slope, slope_out)
    stores.add(hidden.at[0], hidden_a_out)
    stores.add(hidden.at[1], hidden_b_out)
    for at, cols in enumerate(chunks(x.shape[1])):
        downs.wait(at)
        proj[:, cols] = (dot_nn(hidden[0], wd[0, :, cols]) + dot_nn(hidden[1], wd[1, :, cols])).astype(BF)
        stores.add(proj.at[:, cols], proj_out.at[:, cols])
    stores.finish()


def pick_kernel(*refs):
    sources, index, out = refs[:-2], refs[-2], refs[-1]
    choose = one_hot(index[...], len(sources) * ROWS)
    for cols in chunks(out.shape[1]):
        rows = jnp.concatenate([source[:, cols] for source in sources], axis=0)
        out[:, cols] = dot_nn(choose, rows).astype(BF)


def join_kernel(fourth, third, odd, even, own, first_pair, second_pair):
    first_pair[:ROWS, :] = own[...]
    first_pair[ROWS:, :] = even[...] + odd[...]
    second_pair[:ROWS, :] = third[...]
    second_pair[ROWS:, :] = fourth[...]


def finish_kernel(own, other, index, gain_own, gain_other, out, gain_out):
    pick_kernel(own, other, index, out)
    gain_out[...] = gain_own[...] + gain_other[...]


def prepare_kernel(other, index, rows_in, own_in, wide, share, held, sems):
    copies = [pltpu.make_async_copy(ref, held.at[at], sems.at[at]) for at, ref in enumerate((rows_in, own_in))]
    for copy in copies:
        copy.start()
    for copy in copies:
        copy.wait()
    pick_kernel(held.at[1], other, index, share)
    spread_kernel(held.at[0], wide)


def spread_kernel(rows, out):
    for at in range(0, out.shape[0], ROWS):
        out[at : at + ROWS, :] = rows[...]


def cot_kernel(*refs):
    sources, (pick, own_pick, down_a, down_b) = refs[:4], refs[4:8]
    cot_own, cot_out, d_hidden_out, wd, sd, cot, d_hidden, so = refs[8:]
    downs = Weights((down_a, down_b), wd, sd)
    downs.start_all()
    stores = Stores(so)
    choose = one_hot(pick[...], TALL)
    own = one_hot(own_pick[...], TALL)
    total = [None, None]
    for at, cols in enumerate(chunks(cot.shape[1])):
        rows = jnp.concatenate([source[:, cols] for source in sources], axis=0)
        piece = dot_nn(choose, rows).astype(BF)
        cot[:, cols] = piece
        stores.add(cot.at[:, cols], cot_out.at[:, cols])
        cot_own[:, cols] = dot_nn(own, piece).astype(BF)
        downs.wait(at)
        for half in range(2):
            term = dot_nt(piece, wd[half, :, cols])
            total[half] = term if at == 0 else total[half] + term
    for half in range(2):
        d_hidden[half] = total[half].astype(BF)
    stores.add(d_hidden, d_hidden_out)
    stores.finish()


def second_kernel(
    x, gain, own_target, d_hidden_in, up_a, up_b,
    gain_term, own_rows_out, dn_out, normed_out, d_act_a_out, d_act_b_out, hidden_a_out, hidden_b_out,
    wu, su, own_rows, dn, normed, d_act, hidden, d_hidden, sh, so,
):
    ups = Weights((up_a, up_b), wu, su)
    ups.start_all()
    fetch = pltpu.make_async_copy(d_hidden_in, d_hidden, sh)
    fetch.start()
    stores = Stores(so)
    scale = row_scale(x)
    total = normed_times_up(x, scale, gain, normed, normed_out, stores, ups, wu)
    fetch.wait()
    for half in range(2):
        value, slope = silu_parts(total[half])
        hidden[half] = value.astype(BF)
        d_act[half] = (d_hidden[half].astype(F32) * slope).astype(BF)
    stores.add(d_act.at[0], d_act_a_out)
    stores.add(d_act.at[1], d_act_b_out)
    stores.add(hidden.at[0], hidden_a_out)
    stores.add(hidden.at[1], hidden_b_out)
    own = one_hot(own_target[...], TALL)
    for cols in chunks(x.shape[1]):
        own_rows[:, cols] = dot_nn(own, x[:, cols]).astype(BF)
    stores.add(own_rows, own_rows_out)
    for cols in chunks(x.shape[1]):
        term = dot_nn(d_act[0], wu[0, :, cols]) + dot_nn(d_act[1], wu[1, :, cols])
        dn[:, cols] = term.astype(BF)
        stores.add(dn.at[:, cols], dn_out.at[:, cols])
        gain_term[:, cols] = jnp.sum(term * normed[:, cols].astype(F32), axis=0, keepdims=True) / gain[:, cols]
    stores.finish()


def target_kernel(
    to_target, hidden_a, hidden_b, down_a, down_b, near_out, far_out, wd, sd, proj, hidden, sh, so
):
    fetches = [pltpu.make_async_copy(ref, hidden.at[at], sh.at[at]) for at, ref in enumerate((hidden_a, hidden_b))]
    for fetch in fetches:
        fetch.start()
    downs = Weights((down_a, down_b), wd, sd)
    downs.start_all()
    stores = Stores(so)
    sort = one_hot(to_target[...], TALL)
    left = []
    for half, fetch in enumerate(fetches):
        fetch.wait()
        left.append(dot_nn(sort, hidden[half]).astype(BF))
    for at, cols in enumerate(chunks(proj.shape[1])):
        downs.wait(at)
        proj[:, cols] = (dot_nn(left[0], wd[0, :, cols]) + dot_nn(left[1], wd[1, :, cols])).astype(BF)
        stores.add(proj.at[: 4 * ROWS, cols], near_out.at[:, cols])
        stores.add(proj.at[4 * ROWS :, cols], far_out.at[:, cols])
    stores.finish()


def sum_kernel(near, far, mine, second, third, fourth):
    for cols in chunks(near.shape[1]):
        total = near[:, cols].astype(F32) + far[:, cols].astype(F32)
        mine[:, cols] = total[:ROWS]
        for at, out in enumerate((second, third, fourth)):
            out[:, cols] = total[(at + 1) * ROWS : (at + 2) * ROWS].astype(BF)


def second_out_kernel(own_rows, mine, second, third, fourth, out):
    for cols in chunks(out.shape[1]):
        total = mine[:, cols] + second[:, cols].astype(F32) + third[:, cols].astype(F32) + fourth[:, cols].astype(F32)
        out[:, cols] = (own_rows[:, cols].astype(F32) + total).astype(BF)


def first_back_kernel(
    c, gain, gain_two, slope_in, normed_in, d_act_two_b, hidden_one_b, hidden_two_b, up_a, up_b, down_a, down_b,
    dn_out, c_out, d_act_a_out, thin_out,
    wu, wd, su, sd, dn, d_act, slope, normed, thin, sh, so,
):
    width = c.shape[1]
    downs = Weights((down_a, down_b), wd, sd)
    ups = Weights((up_a, up_b), wu, su)
    downs.start_all()
    fetches = [pltpu.make_async_copy(slope_in, slope, sh.at[0]), pltpu.make_async_copy(normed_in, normed, sh.at[1])]
    for at, source in enumerate((d_act_two_b, hidden_one_b, hidden_two_b)):
        fetches.append(pltpu.make_async_copy(source, thin.at[at], sh.at[2 + at]))
    stores = Stores(so)
    total = [None, None]
    for at, cols in enumerate(chunks(width)):
        downs.wait(at)
        if at == 0:
            for fetch in fetches:
                fetch.start()
        ups.start(at)
        for half in range(2):
            term = dot_nt(c[:, cols], wd[half, :, cols])
            total[half] = term if at == 0 else total[half] + term
    for fetch in fetches:
        fetch.wait()
    for half in range(2):
        d_act[half] = (total[half] * slope[half].astype(F32)).astype(BF)
    stores.add(d_act.at[0], d_act_a_out)
    stores.add(c, c_out)
    stores.add(d_act.at[1], thin_out.at[0])
    stores.add(thin, thin_out.at[1:4])
    gain_pieces = []
    for at, cols in enumerate(chunks(width)):
        ups.wait(at)
        term = dot_nn(d_act[0], wu[0, :, cols]) + dot_nn(d_act[1], wu[1, :, cols])
        dn[:, cols] = term.astype(BF)
        stores.add(dn.at[:, cols], dn_out.at[:, cols])
        product = jnp.sum(term * normed[:, cols].astype(F32), axis=0, keepdims=True)
        gain_pieces.append(product / gain[:, cols] + gain_two[:, cols])
    line = jnp.concatenate(gain_pieces, axis=1)
    lanes = width // 8
    grid = jnp.concatenate([line[:, lanes * at : lanes * (at + 1)] for at in range(8)], axis=0)
    high = grid.astype(BF).astype(F32)
    both = jnp.concatenate([high, grid - high], axis=0).astype(BF)
    for block in range(CHIPS):
        dn[block * ROWS : (block + 1) * ROWS, width:] = both
    stores.add(dn.at[:, width:], dn_out.at[:, width:])
    stores.finish()


def add_blocks(blocks, cols):
    total = blocks[0:ROWS, cols].astype(F32)
    for at in range(ROWS, blocks.shape[0], ROWS):
        total = total + blocks[at : at + ROWS, cols].astype(F32)
    return total


def add_kernel(blocks, x, out):
    for cols in chunks(x.shape[1]):
        out[:, cols] = (x[:, cols].astype(F32) + add_blocks(blocks, cols)).astype(BF)


def rows_back_kernel(blocks, x, c, gain, out, spread):
    width = x.shape[1]
    scale = row_scale(x)
    along = jnp.zeros((ROWS, 128), F32)
    for cols in chunks(width):
        piece = add_blocks(blocks, cols) * gain[:, cols]
        spread[:, cols] = piece
        product = piece * (x[:, cols].astype(F32) * scale)
        for at in range(0, CHUNK, 128):
            along = along + product[:, at : at + 128]
    mean = jnp.sum(along, axis=-1, keepdims=True) * (1.0 / width)
    for cols in chunks(width):
        vhat = x[:, cols].astype(F32) * scale
        out[:, cols] = (c[:, cols].astype(F32) + scale * (spread[:, cols] - vhat * mean)).astype(BF)


def last_kernel(blocks, x, c, gain, out, gain_sum, spread):
    width = x.shape[1]
    rows_back_kernel(blocks, x, c, gain, out, spread)
    extra = add_blocks(blocks, slice(width, blocks.shape[1]))
    line = extra[:8] + extra[8:]
    gain_sum[...] = jnp.concatenate([line[at : at + 1] for at in range(8)], axis=1)


def grads_kernel(*refs):
    normed, c, (d_act_one, d_act_two, hidden_one, hidden_two, other) = refs[0:4], refs[4:8], refs[8:13]
    out_up, out_down, left_up, left_down = refs[13:17]

    @pl.when(pl.program_id(0) == 0)
    def _():
        for at, own in enumerate((d_act_one, d_act_two)):
            left_up[:, 2 * at * TALL : (2 * at + 1) * TALL] = own[...].T
            left_up[:, (2 * at + 1) * TALL : (2 * at + 2) * TALL] = other[at].T
        for at, own in enumerate((hidden_one, hidden_two)):
            left_down[:, 2 * at * TALL : (2 * at + 1) * TALL] = own[...].T
            left_down[:, (2 * at + 1) * TALL : (2 * at + 2) * TALL] = other[2 + at].T

    right = jnp.concatenate([ref[...] for ref in normed], axis=0)
    out_up[...] = dot_nn(left_up[...], right).astype(BF)
    right = jnp.concatenate([ref[...] for ref in c], axis=0)
    out_down[...] = dot_nn(left_down[...], right).astype(BF)


def in_vmem(*dims, dtype=BF):
    return pltpu.VMEM(dims, dtype)


def shape(*dims, dtype=BF):
    return jax.ShapeDtypeStruct(dims, dtype)


def in_hbm(value):
    return pltpu.with_memory_space_constraint(value, pltpu.HBM)


def call(kernel, outs, args, from_hbm=(), hbm_outs=(), scratch=(), limit=16, flops=0, moved=0):
    return pl.pallas_call(
        kernel,
        out_shape=list(outs) + [pltpu.HBM(out.shape, out.dtype) for out in hbm_outs],
        in_specs=[VM] * len(args) + [HBM] * len(from_hbm),
        out_specs=[VM] * len(outs) + [HBM] * len(hbm_outs),
        scratch_shapes=scratch,
        compiler_params=pltpu.CompilerParams(vmem_limit_bytes=limit * VMEM_MB),
        cost_estimate=pl.CostEstimate(flops=flops, bytes_accessed=moved, transcendentals=0),
    )(*args, *[in_hbm(value) for value in from_hbm])


def kept(*dims, dtype=BF):
    return pltpu.VMEM(dims, dtype)


def dma(*dims):
    return pltpu.SemaphoreType.DMA(dims)


def weight_scratch(units, width, count):
    return [kept(2, units, width)] * count + [dma(width // CHUNK, 2)] * count


def to_chips(blocks):
    return lax.all_to_all(
        blocks, "peer", split_axis=0, concat_axis=0, tiled=True, axis_index_groups=SAME_CORE
    )


def spread(rows):
    width = rows.shape[1]
    return call(spread_kernel, [in_vmem(TALL, width)], [rows], limit=4, moved=TALL * width * 4)[0]


def from_chips(rows):
    return to_chips(spread(rows))


def swap(value):
    return lax.ppermute(value, "peer", SIBLING)


def after(value, *earlier):
    return lax.optimization_barrier((value,) + earlier)[0]


def together(*values):
    return lax.optimization_barrier(values)


def passed_along(value, steps):
    count = lax.axis_size("section")
    leading, last = (max(0, -steps), min(count, count - steps))
    return lax.ppermute(value, "section", [(source, source + steps) for source in range(leading, last)])


def local(acts, cotangent, gain, w_up, w_down, matching):
    section = lax.axis_index("section")
    peer = lax.axis_index("peer")
    core = peer % 2
    chip = peer // 2
    rows_in, cot_in, up, down = acts[0], cotangent[0], w_up[0], w_down[0]
    units, width = up.shape
    flops = 4 * TALL * units * width
    moved = 2 * TALL * width * 2
    steps = width // CHUNK
    tall, block, slim = shape(TALL, width), shape(ROWS, width), shape(TALL, units)
    both_halves = shape(2, TALL, units)

    cot_b = swap(cot_in)
    up_b, down_b = swap(after(up, cot_b)), swap(after(down, cot_b))

    before = lax.dynamic_index_in_dim(matching, jnp.maximum(section - 1, 0), 0, keepdims=False)
    mine = jnp.where(core == 0, before[0::2], before[1::2])
    chips = jnp.arange(CHIPS, dtype=jnp.int32)
    slots = jnp.arange(ROWS, dtype=jnp.int32)
    pair = jnp.arange(2, dtype=jnp.int32)
    wanted = slots[None, :] ^ mine[:, None]
    apart_y, apart_z = (wanted // 2 - chip) % 4, (wanted // 8) ^ (chip // 4)
    pick = ((apart_z * 4 + apart_y) * ROWS + (wanted % 2) * CHIPS + chips[:, None]).reshape(TALL, 1)
    cot_index = (jnp.where(pair == core, 0, ROWS)[:, None] + 2 * chips[None, :] + core).reshape(ROWS, 1)
    owner = ((chip // 4) ^ pair)[:, None] * 4 + ((chip + jnp.arange(4, dtype=jnp.int32)) % 4)[None, :]
    to_target = (owner.reshape(CHIPS, 1, 1) * 2 + pair[None, :, None]) ^ mine[None, None, :]
    to_target = (to_target + chips[None, None, :] * ROWS).reshape(TALL, 1)
    own_target = to_target[:ROWS]
    own_pick = (chip * ROWS + slots).reshape(ROWS, 1)
    out_index = (jnp.where(slots % 2 == core, 0, ROWS) + core * CHIPS + slots // 2).reshape(ROWS, 1)

    wide_rows, cot_half = call(
        prepare_kernel, [in_vmem(TALL, width), block], [cot_b, cot_index], [rows_in, cot_in], [],
        [kept(2, ROWS, width), dma(2)], limit=8, moved=moved,
    )
    even = lax.ppermute(cot_half, "peer", ALONG_Y[3][0::2])
    wide_rows, even = together(wide_rows, even)
    x_one = to_chips(wide_rows)
    rest = after(cot_half, even)
    fourth, opposite = lax.ppermute(rest, "peer", ALONG_Y[1]), lax.ppermute(rest, "peer", ALONG_Y[2])
    odd = lax.ppermute(rest, "peer", ALONG_Y[3][1::2])
    cot_a, cot_b = call(join_kernel, [shape(2 * ROWS, width)] * 2, [fourth, opposite, odd, even, cot_half], moved=moved)
    x_one, cot_a, cot_b = together(x_one, cot_a, cot_b)
    cot_za = lax.ppermute(cot_a, "peer", ACROSS_Z)
    proj, normed_one, slope_one, hidden_one, hidden_one_b = call(
        forward_kernel, [], [x_one, gain], [up, up_b, down, down_b], [tall, tall, both_halves, slim, slim],
        weight_scratch(units, width, 2)
        + [kept(TALL, width), kept(TALL, width), kept(2, TALL, units), kept(2, TALL, units), dma(2 * steps + 3)],
        limit=36, flops=3 * flops, moved=6 * moved,
    )
    proj, cot_za = together(proj, cot_za)
    blocks = to_chips(proj)
    first = call(add_kernel, [block], [blocks, rows_in], moved=moved)[0]
    arrived = passed_along(first, 1)
    cot_zb = lax.ppermute(after(cot_b, first), "peer", ACROSS_Z)
    arrived, cot_zb = together(arrived, cot_zb)
    cot_all = [cot_a, cot_b, cot_za, cot_zb]
    x_two = from_chips(arrived)
    cot_own, cot, d_hidden = call(
        cot_kernel, [block], cot_all + [pick, own_pick], [down, down_b], [tall, both_halves],
        weight_scratch(units, width, 1) + [kept(TALL, width), kept(2, TALL, units), dma(steps + 1)],
        limit=20, flops=3 * flops, moved=3 * moved,
    )
    gain_two, own_rows, d_normed, normed_two, d_act_two, d_act_two_b, hidden_two, hidden_two_b = call(
        second_kernel, [shape(1, width, dtype=F32)],
        [x_two, gain, own_target], [d_hidden, up, up_b], [block, tall, tall, slim, slim, slim, slim],
        weight_scratch(units, width, 1)
        + [kept(ROWS, width), kept(TALL, width), kept(TALL, width), kept(2, TALL, units), kept(2, TALL, units), kept(2, TALL, units),
           pltpu.SemaphoreType.DMA, dma(2 * steps + 5)],
        limit=28, flops=3 * flops, moved=4 * moved,
    )
    blocks = to_chips(d_normed)
    parts = call(
        target_kernel, [], [to_target], [hidden_two, hidden_two_b, down, down_b],
        [shape(4 * ROWS, width)] * 2,
        weight_scratch(units, width, 1) + [kept(TALL, width), kept(2, TALL, units), dma(2), dma(2 * steps)],
        limit=20, flops=2 * flops, moved=3 * moved,
    )
    blocks = after(blocks, *parts)
    d_two = call(
        rows_back_kernel, [block], [blocks, arrived, cot_own, gain], scratch=[kept(ROWS, width, dtype=F32)], moved=moved
    )[0]
    landed = passed_along(d_two, -1)
    c_all = from_chips(landed)
    near, far, c_all = together(*parts, c_all)
    far = lax.ppermute(far, "peer", ACROSS_Z)
    d_normed, c_one, d_act_one, thin = call(
        first_back_kernel, [], [c_all, gain, gain_two],
        [slope_one, normed_one, d_act_two_b, hidden_one_b, hidden_two_b, up, up_b, down, down_b],
        [shape(TALL, width + width // 8), tall, slim, shape(4, TALL, units)],
        weight_scratch(units, width, 2)
        + [kept(TALL, width + width // 8), kept(2, TALL, units), kept(2, TALL, units), kept(TALL, width), kept(3, TALL, units), dma(5), dma(steps + 5)],
        limit=36, flops=3 * flops, moved=6 * moved,
    )
    ready = d_normed
    d_normed, far = together(d_normed, far)
    blocks = to_chips(d_normed)
    sums = call(sum_kernel, [shape(ROWS, width, dtype=F32), block, block, block], [near, far], moved=moved)
    sums = [sums[0]] + [lax.ppermute(sums[apart], "peer", ALONG_Y[apart]) for apart in (1, 2, 3)]
    wide = []
    for value in (normed_one, normed_two, c_one, cot):
        wide += [value, swap(after(value, ready))]
    slims = [d_act_one, d_act_two, hidden_one, hidden_two, swap(thin)]
    step = 2560
    grad_up, grad_down = pl.pallas_call(
        grads_kernel,
        grid=(width // step,),
        out_shape=[shape(units, width)] * 2,
        in_specs=[pl.BlockSpec((TALL, step), lambda i: (0, i))] * 8
        + [pl.BlockSpec((TALL, units), lambda i: (0, 0))] * 4
        + [pl.BlockSpec((4, TALL, units), lambda i: (0, 0, 0))],
        out_specs=[pl.BlockSpec((units, step), lambda i: (0, i))] * 2,
        scratch_shapes=[kept(units, 4 * TALL)] * 2,
        compiler_params=pltpu.CompilerParams(vmem_limit_bytes=40 * VMEM_MB),
        cost_estimate=pl.CostEstimate(flops=4 * flops, bytes_accessed=8 * moved, transcendentals=0),
    )(*[in_hbm(value) for value in wide], *[in_hbm(value) for value in slims])

    d_one, gain_sum = call(
        last_kernel, [block, shape(1, width, dtype=F32)], [after(blocks, grad_up), rows_in, landed, gain],
        scratch=[kept(ROWS, width, dtype=F32)], moved=moved,
    )
    second = call(second_out_kernel, [block], [after(own_rows, d_one)] + sums, moved=moved // 4)[0]
    second, grad_gain = call(
        finish_kernel, [block, shape(1, width, dtype=F32)],
        [second, swap(second), out_index, gain_sum, swap(gain_sum)],
    )
    return (d_one[None], second[None], grad_up[None], grad_down[None], grad_gain)


def solution(mesh):
    wide = P("section", "peer", None)
    in_specs = (wide, wide, P("section", None), wide, wide, P())
    out_specs = (wide, wide, wide, wide, P("section", None))
    return jax.shard_map(local, mesh=mesh, in_specs=in_specs, out_specs=out_specs, check_vma=False)
```
